128 devices in a mesh: leaf: 16 (over y, z), pts: 8 (over x, core).
Axes of the slice: x: 4, y: 4, z: 4, core: 2. Of those that a mesh axis runs over, the one named last changes fastest.
Arguments:
- vectors: float32 [32, 524288], P(None, ('leaf', 'pts')), may hold values from -6 to 6
- points: float32 [3, 524288], P(None, ('leaf', 'pts')), may hold values from 0 to 1
- leaf_bases: float32 [2048, 64, 256], P(('leaf', 'pts')), may hold values from -0.375 to 0.375
- local_transfer: float32 [128, 30, 64, 64], P(('leaf', 'pts')), may hold values from -0.5 to 0.5
- skel_points: float32 [3, 229376], P(None, ('leaf', 'pts')), may hold values from 0 to 1
- up_transfer: float32 [254, 64, 64], replicated, may hold values from -0.5 to 0.5
- up_points: float32 [3, 16256], replicated, may hold values from 0 to 1
- source_ids: int32 [3, 128, 128, 2], P(None, ('leaf', 'pts')), may hold values from 0 to 2047, as said below
- target_ids: int32 [3, 128, 128, 2], P(None, ('leaf', 'pts')), may hold values from 0 to 2047, as said below
- live_counts: int32 [3, 128, 128], P(None, ('leaf', 'pts')), may hold values from 0 to 2, as said below
Outputs:
- product: float32 [32, 524288], P(None, ('leaf', 'pts'))
The draws below stay inside these ranges and needn't reach their ends.
Inputs may be any that keep to these rules, and one draw needn't show every extreme that they name: source_ids[l, s, d, k] is a node of level l owned by device s: s * (16 / 2**l) + j with j below 16 / 2**l; slots at or past the count hold such ids too. target_ids[l, d, s, k] is a node of level l owned by device d, in the same way. `live_counts`: at each level some device has all 2 slots used from every sending device.
All inputs are finite; a program needn't handle non-finite values.
Results may differ from the reference program's by a relative error of at most 0.0003.
Values sent between devices are 32-bit elements; how exact they have to be, the bound alone decides.
A program may use at most 192 MiB of HBM per device.

```python
import math
import jax
import jax.numpy as jnp
from jax import lax

VEC = 32
RANK = 64
LEAF_PTS = 256
LEAF_DEV = 16
LISTS = 3
CAP = 2
LEAVES = 2048
POINTS = 524288
LOCALN = 30
NODEP = 28
UPN = 254
DEVICES = 128


def pair_tables(key):
    key_source, key_target, key_count, key_full = jax.random.split(key, 4)
    levels_row = jnp.arange(LISTS, dtype=jnp.int32)
    per_level = jnp.right_shift(jnp.full((LISTS,), LEAF_DEV, jnp.int32), levels_row)[:, None, None, None]
    owner = jnp.arange(DEVICES, dtype=jnp.int32)[None, :, None, None]
    raw_source = jax.random.randint(key_source, (LISTS, DEVICES, DEVICES, CAP), 0, LEAF_DEV, dtype=jnp.int32)
    raw_target = jax.random.randint(key_target, (LISTS, DEVICES, DEVICES, CAP), 0, LEAF_DEV, dtype=jnp.int32)
    sources = owner * per_level + raw_source % per_level
    targets = owner * per_level + raw_target % per_level
    counts = jax.random.randint(key_count, (LISTS, DEVICES, DEVICES), 0, CAP + 1, dtype=jnp.int32)
    full_device = jax.random.randint(key_full, (LISTS,), 0, DEVICES, dtype=jnp.int32)
    device_row = jnp.arange(DEVICES, dtype=jnp.int32)[None, :, None]
    counts = jnp.where(device_row == full_device[:, None, None], CAP, counts)
    return (sources, targets, counts)


def draw_source_ids(key, part):
    return pair_tables(key)[0]


def draw_target_ids(key, part):
    return pair_tables(key)[1]


def draw_live_counts(key, part):
    return pair_tables(key)[2]


def block_levels(rng, shape, cuts, least, top_value):
    factor_of = 1.0
    for position, shards_of in cuts:
        draws = jax.random.uniform(jax.random.fold_in(jax.random.fold_in(rng, 6), position), (shards_of,), jnp.float32, least / len(cuts), top_value / len(cuts))
        factor_of = factor_of * jnp.repeat(jnp.exp(draws), shape[position] // shards_of).reshape((-1,) + (1,) * (len(shape) - 1 - position))
    return factor_of


def gaussian(key, shape, spread, most, cuts=(), held_as=jnp.bfloat16):
    loudness = block_levels(key, shape, cuts, -0.22, 0.18) if cuts else 1.0
    values = jax.random.normal(key, shape, jnp.float32) * spread * loudness
    return jnp.minimum(jnp.maximum(values, -most), most).astype(held_as)


def setup_inputs(seed: int = 0) -> dict:
    splits = jax.random.split(jax.random.key(seed), 11)
    vectors = gaussian(splits[0], (VEC, POINTS), 1.0, 6.0, ((1, 128),), jnp.float32)
    points = jnp.clip(1.0 * jax.random.uniform(splits[1], (3, POINTS), jnp.float32) ** block_levels(splits[1], (3, POINTS), ((1, 128),), -0.2, 0.2), 0.0, 1.0)
    leaf_bases = gaussian(splits[2], (LEAVES, RANK, LEAF_PTS), LEAF_PTS ** -0.5, 0.375, ((0, 128),), jnp.float32)
    local_transfer = gaussian(splits[3], (DEVICES, LOCALN, RANK, RANK), (2 * RANK) ** -0.5, 0.5, ((0, 128),), jnp.float32)
    skel_points = jnp.clip(1.0 * jax.random.uniform(splits[4], (3, DEVICES * NODEP * RANK), jnp.float32) ** block_levels(splits[4], (3, DEVICES * NODEP * RANK), ((1, 128),), -0.2, 0.2), 0.0, 1.0)
    up_transfer = gaussian(splits[5], (UPN, RANK, RANK), (2 * RANK) ** -0.5, 0.5, (), jnp.float32)
    up_points = jnp.clip(jax.random.uniform(splits[6], (3, UPN * RANK), jnp.float32, 0.0, 1.0), 0.0, 1.0)
    source_ids = draw_source_ids(jax.random.fold_in(splits[10], 71), 0)
    target_ids = draw_target_ids(jax.random.fold_in(splits[10], 71), 0)
    live_counts = draw_live_counts(jax.random.fold_in(splits[10], 71), 0)
    return dict(vectors=vectors, points=points, leaf_bases=leaf_bases, local_transfer=local_transfer, skel_points=skel_points, up_transfer=up_transfer, up_points=up_points, source_ids=source_ids, target_ids=target_ids, live_counts=live_counts)


PRECISE = lax.Precision.HIGHEST
SCALE_FACTOR = math.sqrt(3.0) / 0.3

def matern(left_pts, right_pts):
    squared = (left_pts[..., 0, :, None] - right_pts[..., 0, None, :]) ** 2
    squared = squared + (left_pts[..., 1, :, None] - right_pts[..., 1, None, :]) ** 2
    squared = squared + (left_pts[..., 2, :, None] - right_pts[..., 2, None, :]) ** 2
    scaled = jnp.sqrt(squared) * SCALE_FACTOR
    return (1.0 + scaled) * jnp.exp(-scaled)

def level_offset(height, count):
    if height == 0:
        return 0
    return 2 * count - (count >> height - 1)

def reference(vectors, points, leaf_bases, local_transfer, skel_points, up_transfer, up_points, source_ids, target_ids, live_counts):
    leaves = LEAF_DEV * DEVICES
    leaf_vectors = vectors.reshape(VEC, leaves, LEAF_PTS)
    coefficients = [jnp.einsum('mip,vmp->mvi', leaf_bases, leaf_vectors, precision=PRECISE)]
    top_local = LEAF_DEV.bit_length() - 1
    matrices = []
    for height in range(top_local):
        node_count = LEAF_DEV >> height
        offset = level_offset(height, LEAF_DEV)
        matrix = local_transfer[:, offset:offset + node_count].reshape(DEVICES * node_count, RANK, RANK)
        moved_up = jnp.einsum('nij,nvj->nvi', matrix, coefficients[-1], precision=PRECISE)
        coefficients.append(moved_up[0::2] + moved_up[1::2])
        matrices.append(matrix)
    upper_levels = DEVICES.bit_length() - 1
    upward = coefficients[-1]
    couples = []
    up_matrices = []
    for height in range(upper_levels):
        node_count = DEVICES >> height
        offset = level_offset(height, DEVICES)
        matrix = up_transfer[offset:offset + node_count]
        node_points = up_points[:, offset * RANK:(offset + node_count) * RANK].reshape(3, node_count, RANK).transpose(1, 0, 2)
        partner = jnp.bitwise_xor(jnp.arange(node_count, dtype=jnp.int32), 1)
        kernel = matern(node_points, node_points[partner])
        couples.append(jnp.einsum('nij,nvj->nvi', kernel, upward[partner], precision=PRECISE))
        up_matrices.append(matrix)
        moved_up = jnp.einsum('nij,nvj->nvi', matrix, upward, precision=PRECISE)
        upward = moved_up[0::2] + moved_up[1::2]
    far_top = couples[-1]
    for height in range(upper_levels - 2, -1, -1):
        far_top = couples[height] + jnp.einsum('nvi,nij->nvj', jnp.repeat(far_top, 2, axis=0), up_matrices[height], precision=PRECISE)
    pts_all = skel_points.reshape(3, DEVICES, NODEP, RANK)
    couplings = []
    for height in range(LISTS):
        node_count = LEAF_DEV >> height
        offset = level_offset(height, LEAF_DEV)
        level_points = pts_all[:, :, offset:offset + node_count].reshape(3, DEVICES * node_count, RANK).transpose(1, 0, 2)
        level_coefs = coefficients[height]

        def per_device(inputs):
            dest_index, source_row, target_row, count_row = inputs
            kernel = matern(level_points[target_row], level_points[source_row])
            products = jnp.einsum('scij,scvj->scvi', kernel, level_coefs[source_row], precision=PRECISE)
            live_mask = (jnp.arange(CAP, dtype=jnp.int32)[None, :] < count_row[:, None]).astype(jnp.float32)
            products = products * live_mask[:, :, None, None]
            local_ids = (target_row - dest_index * node_count).reshape(-1).astype(jnp.int32)
            return jnp.zeros((node_count, VEC, RANK), jnp.float32).at[local_ids].add(products.reshape(-1, VEC, RANK))
        gathered = lax.map(per_device, (jnp.arange(DEVICES, dtype=jnp.int32), jnp.transpose(source_ids[height], (1, 0, 2)), target_ids[height], live_counts[height]))
        couplings.append(gathered.reshape(DEVICES * node_count, VEC, RANK))
    downward = far_top
    if top_local < LISTS:
        downward = downward + couplings[top_local]
    for height in range(top_local - 1, -1, -1):
        downward = jnp.einsum('nvi,nij->nvj', jnp.repeat(downward, 2, axis=0), matrices[height], precision=PRECISE)
        if height < LISTS:
            downward = downward + couplings[height]
    far_field = jnp.einsum('mip,mvi->mvp', leaf_bases, downward, precision=PRECISE)
    leaf_points = points.reshape(3, leaves, LEAF_PTS).transpose(1, 0, 2)
    padded_points = jnp.pad(leaf_points, ((1, 1), (0, 0), (0, 0)))
    padded_vectors = jnp.pad(leaf_vectors.transpose(1, 0, 2), ((1, 1), (0, 0), (0, 0)))

    def near_leaf(leaf_index):
        near_points = lax.dynamic_slice_in_dim(padded_points, leaf_index, 3, 0).transpose(1, 0, 2).reshape(3, 3 * LEAF_PTS)
        near_vectors = lax.dynamic_slice_in_dim(padded_vectors, leaf_index, 3, 0).transpose(1, 0, 2).reshape(VEC, 3 * LEAF_PTS)
        kernel = matern(leaf_points[leaf_index], near_points)
        return jnp.dot(near_vectors, kernel.T, precision=PRECISE)
    near_field = lax.map(near_leaf, jnp.arange(leaves, dtype=jnp.int32))
    result = (near_field + far_field).transpose(1, 0, 2).reshape(VEC, leaves * LEAF_PTS)
    return result
```

```python
import functools
import math

import jax
import jax.numpy as jnp
from jax import lax
from jax.experimental import pallas as pl
from jax.experimental.pallas import tpu as pltpu
from jax.sharding import PartitionSpec as P

F32 = jnp.float32
BF16 = jnp.bfloat16
MESH = pl.DeviceIdType.MESH
LN2 = math.log(2.0)
KAPPA = math.sqrt(3.0) / 0.3 / LN2
TINY = 1e-30

VEC = 32
RANK = 64
LEAF = 256
LEAVES = 16
PTS = 8
LEAFS = 16
PAIRS = 14
NODES = 28
COEF_ROWS = PAIRS * VEC
PAY_ROWS = COEF_ROWS + PAIRS * 8
UPPER = 7
NN = (((1,), (0,)), ((), ()))
NT = (((1,), (1,)), ((), ()))


def dg(a, b, dims):
    return lax.dot_general(a, b, dims, preferred_element_type=F32)


def split(x):
    hi = x.astype(BF16)
    return hi, (x - hi.astype(F32)).astype(BF16)


def dot3(a, b, dims):
    ah, al = split(a)
    bh, bl = split(b)
    return dg(ah, bh, dims) + (dg(ah, bl, dims) + dg(al, bh, dims))


def split3(x):
    h = x.astype(BF16).astype(F32)
    r = x - h
    m = r.astype(BF16).astype(F32)
    return h, m, r - m


def forms(pts):
    n = pts.shape[1]
    x = (pts - 0.5) * KAPPA
    x = jnp.concatenate([x, jnp.zeros((5, n), F32)], axis=0)
    q = jnp.sum(x * x, axis=0, keepdims=True)
    row = lax.broadcasted_iota(jnp.int32, (8, n), 0)
    w = jnp.where(row < 3, x, jnp.where(row == 3, 1.0, jnp.where(row == 4, q, 0.0)))
    u = jnp.where(row < 3, -2.0 * x, jnp.where(row == 3, q, jnp.where(row == 4, 1.0, 0.0)))
    return u, w


def stack_u(u):
    h, m, l = split3(u)
    z = jnp.zeros_like(h)
    return jnp.concatenate([h, h, m, m, h, l, z, z], axis=0)


def stack_w(w):
    h, m, l = split3(w)
    z = jnp.zeros_like(h)
    return jnp.concatenate([h, m, h, m, l, h, z, z], axis=0)


def matern(squared):
    squared = jnp.maximum(squared, TINY)
    t = squared * lax.rsqrt(squared)
    return (1.0 + LN2 * t) * jnp.exp2(-t)


def pair_matrix(lt_ref, n):
    return jnp.concatenate([lt_ref[2 * n], lt_ref[2 * n + 1]], axis=1)


def up_offset(u):
    return 0 if u == 0 else 256 - (128 >> (u - 1))


def gather_kernel(
    vec_ref, pts_ref, base_ref, lt_ref, skel_ref, upt_ref, upp_ref, sc_ref, tc_ref,
    g_ref, near_ref, far_ref, tp_ref, scg_ref, tcg_ref,
    u_scr, w_scr, v_scr, halo_src, halo_dst, pay, tpay, ut, xs, xr, sf,
    ssem, rsem, lsem,
):
    leaf = lax.axis_index("leaf")
    p = lax.axis_index("pts")
    me = leaf * PTS + p
    y = leaf // 4
    z = lax.rem(leaf, 4)
    nxt = lax.rem(me + 1, 128)
    prv = lax.rem(me + 127, 128)
    nxt_dev = (nxt // PTS, lax.rem(nxt, PTS))
    prv_dev = (prv // PTS, lax.rem(prv, PTS))

    barrier = pltpu.get_barrier_semaphore()
    for k in range(1, LEAFS):
        pl.semaphore_signal(barrier, inc=1, device_id=(leaf ^ k, p), device_id_type=MESH)
    for k in range(1, PTS):
        pl.semaphore_signal(barrier, inc=1, device_id=(leaf, p ^ k), device_id_type=MESH)
    pl.semaphore_signal(barrier, inc=1, device_id=nxt_dev, device_id_type=MESH)
    pl.semaphore_signal(barrier, inc=1, device_id=prv_dev, device_id_type=MESH)

    counter = [0]
    sends = []

    def remote(src, dst, dev):
        i = counter[0]
        counter[0] += 1
        copy = pltpu.make_async_remote_copy(
            src_ref=src, dst_ref=dst, send_sem=ssem.at[i], recv_sem=rsem.at[i],
            device_id=dev, device_id_type=MESH,
        )
        copy.start()
        sends.append(copy)
        return copy

    locals_ = []

    def local(src, dst):
        copy = pltpu.make_async_copy(src, dst, lsem.at[len(locals_)])
        copy.start()
        locals_.append(copy)

    for u in range(UPPER):
        first = lax.shift_right_logical(me, u + 1) * 2
        local(upt_ref.at[pl.ds(up_offset(u) + first, 2)], ut.at[u])

    for side, off in ((0, 0), (1, (LEAVES - 1) * LEAF)):
        halo_src[side, 0:VEC] = vec_ref[:, off:off + LEAF]
        halo_src[side, VEC:VEC + 8] = jnp.concatenate(
            [pts_ref[:, off:off + LEAF], jnp.zeros((5, LEAF), F32)], axis=0
        )
    for a in range(PAIRS):
        u8, w8 = forms(skel_ref[:, a * 128:(a + 1) * 128])
        tpay[a * 8:(a + 1) * 8] = u8
        pay[COEF_ROWS + a * 8:COEF_ROWS + (a + 1) * 8] = w8

    pl.semaphore_wait(barrier, LEAFS + PTS)

    h0 = remote(halo_src.at[0], halo_dst.at[1], prv_dev)
    h1 = remote(halo_src.at[1], halo_dst.at[0], nxt_dev)
    arrivals = []
    for k in range(1, PTS):
        arrivals.append(remote(tpay, tp_ref.at[p], (leaf, p ^ k)))
        arrivals.append(remote(tc_ref, tcg_ref.at[p], (leaf, p ^ k)))
    for k in range(1, LEAFS):
        arrivals.append(remote(sc_ref, scg_ref.at[leaf], (leaf ^ k, p)))
    local(tpay, tp_ref.at[p])
    local(tc_ref, tcg_ref.at[p])
    local(sc_ref, scg_ref.at[leaf])

    pairs = []
    for m in range(LEAVES // 2):
        both = []
        for j in range(2):
            n = 2 * m + j
            both.append(dot3(vec_ref[:, n * LEAF:(n + 1) * LEAF], base_ref[n], NT))
        pairs.append(jnp.concatenate(both, axis=1))
    base = 0
    row = 0
    root = None
    while True:
        if row < COEF_ROWS:
            for c in pairs:
                pay[row:row + VEC] = c
                row += VEC
        ups = [dot3(c, pair_matrix(lt_ref, base + i), NT) for i, c in enumerate(pairs)]
        base += len(pairs)
        if len(ups) == 1:
            root = ups[0]
            break
        pairs = [
            jnp.concatenate([ups[2 * i], ups[2 * i + 1]], axis=1) for i in range(len(ups) // 2)
        ]

    half = PAY_ROWS // 2
    quarter = 136

    def lid(yy, zz):
        return lax.rem(yy + 4, 4) * 4 + lax.rem(zz + 4, 4)

    def near_id(h, stage, step):
        return lid(y, z + step) if (h == 0) == (stage == 0) else lid(y + step, z)

    def block_id(h, first, second):
        return lid(y + second, z + first) if h == 0 else lid(y + first, z + second)

    stage1 = {}
    stage2 = {}
    for h in range(2):
        rows = pl.ds(h * half, half)
        for step in (1, -1):
            stage1[h, step] = remote(
                pay.at[rows], g_ref.at[leaf, rows], (near_id(h, 0, step), p)
            )

    def spread(h, first):
        rows = pl.ds(h * half, half)
        blk = near_id(h, 0, first)
        src = pay.at[rows] if first == 0 else g_ref.at[blk, rows]
        for step in (1, -1):
            stage2[h, first, step] = remote(
                src, g_ref.at[blk, rows], (near_id(h, 1, step), p)
            )

    for h in range(2):
        spread(h, 0)
    local(pay, g_ref.at[leaf])

    def forward(h, stage, blk_minus, blk_plus, got_minus, got_plus):
        got_minus.wait_recv()
        rows = pl.ds(h * half, quarter)
        one = remote(g_ref.at[blk_minus, rows], g_ref.at[blk_minus, rows], (near_id(h, stage, 1), p))
        got_plus.wait_recv()
        rows = pl.ds(h * half + quarter, half - quarter)
        two = remote(g_ref.at[blk_plus, rows], g_ref.at[blk_plus, rows], (near_id(h, stage, -1), p))
        return one, two

    opposite = {}

    def step_a():
        for h in range(2):
            opposite[h] = forward(
                h, 0, near_id(h, 0, -1), near_id(h, 0, 1), stage1[h, 1], stage1[h, -1]
            )
            spread(h, -1)
            spread(h, 1)

    def step_b():
        for h in range(2):
            opposite[h][0].wait_recv()
            opposite[h][1].wait_recv()
            spread(h, 2)

    last = []

    def step_c(first):
        for h in range(2):
            last.extend(
                forward(
                    h, 1, block_id(h, first, -1), block_id(h, first, 1),
                    stage2[h, first, 1], stage2[h, first, -1],
                )
            )

    upward = {}

    def send_up(u, value):
        xs[u] = value
        dev = (leaf, p ^ (1 << u)) if u < 3 else (leaf ^ (1 << (u - 3)), p)
        upward[u] = remote(xs.at[u], xr.at[u], dev)

    send_up(0, root)

    def climb(u):
        upward[u].wait_recv()
        locals_[u].wait()
        node = lax.shift_right_logical(me, u)
        left_side = lax.rem(node, 2) == 0
        own = xs[u]
        sib = xr[u]
        pair = jnp.concatenate(
            [jnp.where(left_side, own, sib), jnp.where(left_side, sib, own)], axis=1
        )
        if u < UPPER - 1:
            mat = jnp.concatenate([ut[u, 0], ut[u, 1]], axis=1)
            send_up(u + 1, dot3(pair, mat, NT))
        col = pl.multiple_of((up_offset(u) + (node // 2) * 2) * RANK, 128)
        u8, w8 = forms(upp_ref[:, pl.ds(col, 128)])
        kern = matern(dg(stack_u(u8).T.astype(BF16), stack_w(w8).astype(BF16), NN))
        lane_left = lax.broadcasted_iota(jnp.int32, (VEC, 2 * RANK), 1) < RANK
        only_sib = jnp.where(jnp.logical_xor(lane_left, left_side), pair, 0.0)
        out = dot3(only_sib, kern, NN)
        sf[u] = jnp.where(left_side, out[:, :RANK], out[:, RANK:])

    def prepare(slot, vec, pts):
        vh, vl = split(vec)
        lanes = pl.ds(pl.multiple_of(slot * LEAF, LEAF), LEAF)
        v_scr[0:VEC, lanes] = vh
        v_scr[VEC:2 * VEC, lanes] = vl
        u8, w8 = forms(pts)
        w_scr[:, lanes] = stack_w(w8).astype(BF16)
        u_scr[lanes, :] = stack_u(u8).T.astype(BF16)

    @pl.loop(0, LEAVES)
    def _(m):
        lanes = pl.ds(pl.multiple_of(m * LEAF, LEAF), LEAF)
        prepare(m + 1, vec_ref[:, lanes], pts_ref[:, lanes])

    def near(m):
        lanes = pl.ds(pl.multiple_of(m * LEAF, LEAF), LEAF)
        w = w_scr[:, lanes]
        total = None
        for b in range(3):
            src = pl.ds(pl.multiple_of((m - 1 + b) * LEAF, LEAF), LEAF)
            kh, kl = split(matern(dg(u_scr[src, :], w, NN)))
            v = v_scr[:, src]
            big = dg(v, kh, NN)
            part = big[:VEC] + (big[VEC:] + dg(v[:VEC], kl, NN))
            total = part if total is None else total + part
        near_ref[:, pl.ds(pl.multiple_of((m - 1) * LEAF, LEAF), LEAF)] = total

    def near_span(lo, hi):
        @pl.loop(lo, hi)
        def _(m):
            near(m)

    step_a()
    climb(0)
    near_span(2, 3)
    climb(1)
    near_span(3, 4)
    step_b()
    climb(2)
    near_span(4, 6)
    step_c(0)
    climb(3)
    near_span(6, 8)
    climb(4)
    near_span(8, 10)
    step_c(-1)
    climb(5)
    near_span(10, 12)
    step_c(1)
    climb(6)
    near_span(12, 14)
    step_c(2)
    near_span(14, 16)
    h0.wait_recv()
    h1.wait_recv()
    for side, slot, edge in ((0, 0, 0), (1, LEAVES + 1, 127)):
        vec = jnp.where(me == edge, 0.0, halo_dst[side, 0:VEC])
        prepare(slot, vec, halo_dst[side, VEC:VEC + 3])
    near(1)
    near(LEAVES)

    far = sf[UPPER - 1]
    for u in range(UPPER - 2, -1, -1):
        left_side = lax.rem(lax.shift_right_logical(me, u), 2) == 0
        mat = jnp.where(left_side, ut[u, 0], ut[u, 1])
        far = sf[u] + dot3(far, mat, NN)
    far_ref[...] = far

    for c in arrivals:
        c.wait_recv()
    for c in last:
        c.wait_recv()
    for c in sends:
        c.wait_send()
    for c in locals_[UPPER:]:
        c.wait()


def couple_kernel(g_ref, tp_ref, sc_ref, tc_ref, o_ref, ca, cb, wa, wb, ua, ub, acc_a, acc_b):
    leaf = lax.axis_index("leaf")
    p = lax.axis_index("pts")
    low = lax.broadcasted_iota(jnp.int32, (VEC, 128), 1) < RANK
    low_w = lax.broadcasted_iota(jnp.int32, (64, 128), 1) < RANK

    @pl.loop(0, LEAFS)
    def _(s):
        for a in range(PAIRS):
            c = g_ref[s, a * VEC:(a + 1) * VEC, :]
            h = c.astype(BF16).astype(F32)
            l = c - h
            node = s * NODES + 2 * a
            w = stack_w(g_ref[s, COEF_ROWS + a * 8:COEF_ROWS + (a + 1) * 8, :])
            wr = pltpu.roll(w, RANK, 1)
            for j in range(2):
                rows = pl.ds(pl.multiple_of((node + j) * 64, 64), 64)
                cur, oth = (w, wr) if j == 0 else (wr, w)
                wa[rows, :] = jnp.where(low_w, cur, 0.0).astype(BF16)
                wb[rows, :] = jnp.where(low_w, 0.0, oth).astype(BF16)
            x = jnp.concatenate([h, l], axis=0)
            xr = pltpu.roll(x, RANK, 1)
            for j in range(2):
                rows = pl.ds(pl.multiple_of((node + j) * 64, 64), 64)
                cur, oth = (x, xr) if j == 0 else (xr, x)
                ca[rows, :] = jnp.where(low_w, cur, 0.0).astype(BF16)
                cb[rows, :] = jnp.where(low_w, 0.0, oth).astype(BF16)

    @pl.loop(0, PTS)
    def _(d):
        zero = jnp.zeros((64, 64), F32)
        for a in range(PAIRS):
            t = stack_u(tp_ref[d, a * 8:(a + 1) * 8, :]).T
            for j in range(2):
                rows = pl.ds(pl.multiple_of((d * 32 + 2 * a + j) * 64, 64), 64)
                part = t[j * 64:(j + 1) * 64]
                ua[rows, :] = jnp.concatenate([part, zero], axis=1).astype(BF16)
                ub[rows, :] = jnp.concatenate([zero, part], axis=1).astype(BF16)
        rows = pl.ds(pl.multiple_of((d * 32 + NODES) * 64, 64), 64)
        ua[rows, :] = jnp.zeros((64, 128), BF16)
        ub[rows, :] = jnp.zeros((64, 128), BF16)
        rows = pl.ds(pl.multiple_of(d * 32 * VEC, 32), 32 * VEC)
        acc_a[rows, :] = jnp.zeros((32 * VEC, RANK), F32)
        acc_b[rows, :] = jnp.zeros((32 * VEC, RANK), F32)

    @pl.loop(0, PTS * 3)
    def _(g):
        d = g // 3
        lev = lax.rem(g, 3)
        outs = []
        for s in range(LEAFS):
            na = s * NODES + sc_ref[s, lev * 2, leaf * PTS + d]
            nb = s * NODES + sc_ref[s, lev * 2 + 1, leaf * PTS + d]
            ra = d * 32 + tc_ref[d, lev * 2, s * PTS + p]
            rb = d * 32 + tc_ref[d, lev * 2 + 1, s * PTS + p]
            na = pl.multiple_of(na * 64, 64)
            nb = pl.multiple_of(nb * 64, 64)
            u = ua[pl.ds(pl.multiple_of(ra * 64, 64), 64), :] + ub[pl.ds(pl.multiple_of(rb * 64, 64), 64), :]
            w = jnp.concatenate([wa[pl.ds(na, 64), :], wb[pl.ds(nb, 64), :]], axis=0)
            kh, kl = split(matern(dg(u, w, NN)))
            xa = ca[pl.ds(na, 64), :]
            xb = cb[pl.ds(nb, 64), :]
            one = dg(jnp.concatenate([xa, xb], axis=0), kh, NT)
            two = dg(jnp.concatenate([xa[:VEC], xb[:VEC]], axis=0), kl, NT)
            outs.append((
                ra, rb,
                one[0:32] + (one[32:64] + two[0:32]),
                one[64:96] + (one[96:128] + two[32:64]),
            ))
        for ra, rb, pa, pb in outs:
            acc_a[pl.ds(pl.multiple_of(ra * VEC, VEC), VEC), :] += pa
            acc_b[pl.ds(pl.multiple_of(rb * VEC, VEC), VEC), :] += pb

    @pl.loop(0, PTS)
    def _(d):
        for a in range(PAIRS):
            both = []
            for j in range(2):
                rows = pl.ds(pl.multiple_of((d * 32 + 2 * a + j) * VEC, VEC), VEC)
                both.append(acc_a[rows, :] + acc_b[rows, :])
            o_ref[d, a * VEC:(a + 1) * VEC, :] = jnp.concatenate(both, axis=1)


def scatter_kernel(acc_ref, far_ref, lt_ref, base_ref, near_ref, out_ref, from_core, s1, s2, work, ssem, rsem):
    leaf = lax.axis_index("leaf")
    p = lax.axis_index("pts")
    x = p // 2
    core = lax.rem(p, 2)
    sister = (leaf, p ^ 1)

    def dev(step):
        return (leaf, lax.rem(x + step + 4, 4) * 2 + core)

    barrier = pltpu.get_barrier_semaphore()
    for d in (sister, dev(1), dev(-1)):
        pl.semaphore_signal(barrier, inc=1, device_id=d, device_id_type=MESH)
    pl.semaphore_wait(barrier, 3)

    sends = []

    def remote(src, dst, device):
        i = len(sends)
        copy = pltpu.make_async_remote_copy(
            src_ref=src, dst_ref=dst, send_sem=ssem.at[i], recv_sem=rsem.at[i],
            device_id=device, device_id_type=MESH,
        )
        copy.start()
        sends.append(copy)
        return copy

    half = COEF_ROWS // 2
    steps = (2, 1, 3, 0)
    first = {}
    for st in steps:
        xx = lax.rem(x + st, 4)
        first[st] = remote(acc_ref.at[xx * 2 + 1 - core], from_core.at[st], sister)

    def summed(st):
        first[st].wait_recv()
        return acc_ref[lax.rem(x + st, 4) * 2 + core] + from_core[st]

    work[0] = summed(2)
    a1 = remote(work.at[0, pl.ds(0, half)], s1.at[pl.ds(0, half)], dev(1))
    b1 = remote(work.at[0, pl.ds(half, half)], s1.at[pl.ds(half, half)], dev(-1))
    work[1] = summed(1)
    work[2] = summed(3)
    a1.wait_recv()
    work[1, 0:half] += s1[0:half]
    a2 = remote(work.at[1], s2.at[0], dev(1))
    b1.wait_recv()
    work[2, half:] += s1[half:]
    b2 = remote(work.at[2], s2.at[1], dev(-1))

    def down(node, n):
        return dot3(node, pair_matrix(lt_ref, n), NN)

    top = down(far_ref[...], 14)
    level2 = [down(top[:, :RANK], 12), down(top[:, RANK:], 13)]
    own = summed(0)
    a2.wait_recv()
    b2.wait_recv()
    work[3] = own + (s2[0] + s2[1])

    def coupling(a):
        return work[3, a * VEC:(a + 1) * VEC]

    pairs = [level2[i] + coupling(12 + i) for i in range(2)]
    pairs = [
        down(pairs[i // 2][:, (i % 2) * RANK:(i % 2 + 1) * RANK], 8 + i) + coupling(8 + i)
        for i in range(4)
    ]
    pairs = [
        down(pairs[i // 2][:, (i % 2) * RANK:(i % 2 + 1) * RANK], i) + coupling(i)
        for i in range(8)
    ]
    for m in range(LEAVES):
        c = pairs[m // 2][:, (m % 2) * RANK:(m % 2 + 1) * RANK]
        cols = slice(m * LEAF, (m + 1) * LEAF)
        out_ref[:, cols] = near_ref[:, cols] + dot3(c, base_ref[m], NN)
    for c in sends:
        c.wait_send()


def vmem():
    return pl.BlockSpec(memory_space=pltpu.VMEM)


def smem():
    return pl.BlockSpec(memory_space=pltpu.SMEM)


def anywhere():
    return pl.BlockSpec(memory_space=pl.ANY)


def shape(*dims, dtype=F32):
    return jax.ShapeDtypeStruct(dims, dtype)


def on_device(
    vectors, points, leaf_bases, local_transfer, skel_points, up_transfer, up_points,
    source_ids, target_ids, live_counts,
):
    me = lax.axis_index("leaf") * PTS + lax.axis_index("pts")
    counts = jnp.array([LEAVES, LEAVES // 2, LEAVES // 4], jnp.int32)
    starts = jnp.array([0, LEAVES, LEAVES + LEAVES // 2], jnp.int32)
    shift = (starts - me * counts)[:, None, None]
    slot = jnp.arange(2, dtype=jnp.int32)
    source_code = jnp.swapaxes(source_ids[:, 0], 1, 2) + shift
    target_code = jnp.where(
        slot[None, :, None] < live_counts[:, 0, None, :],
        jnp.swapaxes(target_ids[:, 0], 1, 2) + shift,
        NODES,
    )
    source_code = jnp.pad(source_code.reshape(6, 128), ((0, 2), (0, 0)))
    target_code = jnp.pad(target_code.reshape(6, 128), ((0, 2), (0, 0)))
    lt = local_transfer[0]
    n_remote = 96

    gathered, near, far, tp, scg, tcg = pl.pallas_call(
        gather_kernel,
        out_shape=(
            shape(LEAFS, PAY_ROWS, 128), shape(VEC, LEAVES * LEAF), shape(VEC, RANK),
            shape(PTS, PAIRS * 8, 128), shape(LEAFS, 8, 128, dtype=jnp.int32),
            shape(PTS, 8, 128, dtype=jnp.int32),
        ),
        in_specs=[vmem()] * 5 + [anywhere()] + [vmem()] * 3,
        out_specs=(vmem(),) * 6,
        scratch_shapes=[
            pltpu.VMEM((18 * LEAF, 64), BF16),
            pltpu.VMEM((64, 18 * LEAF), BF16),
            pltpu.VMEM((2 * VEC, 18 * LEAF), BF16),
            pltpu.VMEM((2, VEC + 8, LEAF), F32),
            pltpu.VMEM((2, VEC + 8, LEAF), F32),
            pltpu.VMEM((PAY_ROWS, 128), F32),
            pltpu.VMEM((PAIRS * 8, 128), F32),
            pltpu.VMEM((UPPER, 2, RANK, RANK), F32),
            pltpu.VMEM((UPPER, VEC, RANK), F32),
            pltpu.VMEM((UPPER, VEC, RANK), F32),
            pltpu.VMEM((UPPER, VEC, RANK), F32),
            pltpu.SemaphoreType.DMA((n_remote,)),
            pltpu.SemaphoreType.DMA((n_remote,)),
            pltpu.SemaphoreType.DMA((16,)),
        ],
        compiler_params=pltpu.CompilerParams(
            collective_id=0, has_side_effects=True, vmem_limit_bytes=48 << 20
        ),
    )(vectors, points, leaf_bases, lt, skel_points, up_transfer, up_points, source_code, target_code)

    partial = pl.pallas_call(
        couple_kernel,
        out_shape=shape(PTS, COEF_ROWS, 128),
        in_specs=[vmem(), vmem(), smem(), smem()],
        out_specs=vmem(),
        scratch_shapes=[
            pltpu.VMEM((LEAFS * NODES * 64, 128), BF16),
            pltpu.VMEM((LEAFS * NODES * 64, 128), BF16),
            pltpu.VMEM((LEAFS * NODES * 64, 128), BF16),
            pltpu.VMEM((LEAFS * NODES * 64, 128), BF16),
            pltpu.VMEM((PTS * 32 * 64, 128), BF16),
            pltpu.VMEM((PTS * 32 * 64, 128), BF16),
            pltpu.VMEM((PTS * 32 * VEC, RANK), F32),
            pltpu.VMEM((PTS * 32 * VEC, RANK), F32),
        ],
        compiler_params=pltpu.CompilerParams(vmem_limit_bytes=56 << 20),
    )(gathered, tp, scg, tcg)

    return pl.pallas_call(
        scatter_kernel,
        out_shape=shape(VEC, LEAVES * LEAF),
        in_specs=[vmem()] * 5,
        out_specs=vmem(),
        scratch_shapes=[
            pltpu.VMEM((4, COEF_ROWS, 128), F32),
            pltpu.VMEM((COEF_ROWS, 128), F32),
            pltpu.VMEM((2, COEF_ROWS, 128), F32),
            pltpu.VMEM((4, COEF_ROWS, 128), F32),
            pltpu.SemaphoreType.DMA((8,)),
            pltpu.SemaphoreType.DMA((8,)),
        ],
        compiler_params=pltpu.CompilerParams(
            collective_id=1, has_side_effects=True, vmem_limit_bytes=48 << 20
        ),
    )(partial, far, lt, leaf_bases, near)


def solution(mesh):
    both = ("leaf", "pts")
    return jax.shard_map(
        on_device,
        mesh=mesh,
        in_specs=(
            P(None, both),
            P(None, both),
            P(both, None, None),
            P(both, None, None, None),
            P(None, both),
            P(),
            P(),
            P(None, both, None, None),
            P(None, both, None, None),
            P(None, both, None),
        ),
        out_specs=P(None, both),
        check_vma=False,
    )
```

```python
import functools
import math

import jax
import jax.numpy as jnp
from jax import lax
from jax.experimental import pallas as pl
from jax.experimental.pallas import tpu as pltpu
from jax.sharding import PartitionSpec as P

F32 = jnp.float32
BF16 = jnp.bfloat16
MESH = pl.DeviceIdType.MESH
LN2 = math.log(2.0)
KAPPA = math.sqrt(3.0) / 0.3 / LN2
TINY = 1e-30

VEC = 32
RANK = 64
LEAF = 256
LEAVES = 16
PTS = 8
LEAFS = 16
PAIRS = 14
NODES = 28
COEF_ROWS = PAIRS * VEC
PAY_ROWS = COEF_ROWS + 48
UPPER = 7
UPN = 254
GROUPS = NODES // 4
DEPTH = 48
NN = (((1,), (0,)), ((), ()))
NT = (((1,), (1,)), ((), ()))


def dg(a, b, dims):
    return lax.dot_general(a, b, dims, preferred_element_type=F32)


def split(x):
    hi = x.astype(BF16)
    return hi, (x - hi.astype(F32)).astype(BF16)


def dot3(a, b, dims):
    ah, al = split(a)
    bh, bl = split(b)
    return dg(ah, bh, dims) + (dg(ah, bl, dims) + dg(al, bh, dims))


def split3(x):
    h = x.astype(BF16).astype(F32)
    r = x - h
    m = r.astype(BF16).astype(F32)
    return h, m, r - m


def scaled(pts):
    return (pts - 0.5) * KAPPA


def forms(x):
    n = x.shape[1]
    x = jnp.concatenate([x, jnp.zeros((5, n), F32)], axis=0)
    q = jnp.sum(x * x, axis=0, keepdims=True)
    row = lax.broadcasted_iota(jnp.int32, (8, n), 0)
    w = jnp.where(row < 3, x, jnp.where(row == 3, 1.0, jnp.where(row == 4, q, 0.0)))
    u = jnp.where(row < 3, -2.0 * x, jnp.where(row == 3, q, jnp.where(row == 4, 1.0, 0.0)))
    return u, w


def stack_u(u):
    h, m, l = split3(u)
    return jnp.concatenate([h, h, m, m, h, l], axis=0)


def stack_w(w):
    h, m, l = split3(w)
    return jnp.concatenate([h, m, h, m, l, h], axis=0)


def matern(squared):
    squared = jnp.maximum(squared, TINY)
    t = squared * lax.rsqrt(squared)
    return (1.0 + LN2 * t) * jnp.exp2(-t)


def pair_matrix(lt_ref, n):
    return jnp.concatenate([lt_ref[2 * n], lt_ref[2 * n + 1]], axis=1)


def up_offset(u):
    return 0 if u == 0 else 256 - (128 >> (u - 1))


def gather_kernel(
    vec_ref, pts_ref, base_ref, lt_ref, skel_ref, upt_ref, upp_ref, sc_ref, tc_ref,
    g_ref, near_ref, far_ref, tp_ref, scg_ref, tcg_ref,
    u_scr, w_scr, v_scr, halo_src, halo_dst, pay, tpay, up_all, ut, xs, xr, sf,
    ssem, rsem, lsem,
):
    leaf = lax.axis_index("leaf")
    p = lax.axis_index("pts")
    me = leaf * PTS + p
    y = leaf // 4
    z = lax.rem(leaf, 4)
    nxt = lax.rem(me + 1, 128)
    prv = lax.rem(me + 127, 128)
    nxt_dev = (nxt // PTS, lax.rem(nxt, PTS))
    prv_dev = (prv // PTS, lax.rem(prv, PTS))

    barrier = pltpu.get_barrier_semaphore()
    for k in range(1, LEAFS):
        pl.semaphore_signal(barrier, inc=1, device_id=(leaf ^ k, p), device_id_type=MESH)
    for k in range(1, PTS):
        pl.semaphore_signal(barrier, inc=1, device_id=(leaf, p ^ k), device_id_type=MESH)
    pl.semaphore_signal(barrier, inc=1, device_id=nxt_dev, device_id_type=MESH)
    pl.semaphore_signal(barrier, inc=1, device_id=prv_dev, device_id_type=MESH)

    counter = [0]
    sends = []

    def remote(src, dst, dev):
        i = counter[0]
        counter[0] += 1
        copy = pltpu.make_async_remote_copy(
            src_ref=src, dst_ref=dst, send_sem=ssem.at[i], recv_sem=rsem.at[i],
            device_id=dev, device_id_type=MESH,
        )
        copy.start()
        sends.append(copy)
        return copy

    locals_ = []

    def local(src, dst):
        copy = pltpu.make_async_copy(src, dst, lsem.at[len(locals_)])
        copy.start()
        locals_.append(copy)

    local(upt_ref, up_all)

    for side, off in ((0, 0), (1, (LEAVES - 1) * LEAF)):
        halo_src[side, 0:VEC] = vec_ref[:, off:off + LEAF]
        halo_src[side, VEC:VEC + 8] = jnp.concatenate(
            [pts_ref[:, off:off + LEAF], jnp.zeros((5, LEAF), F32)], axis=0
        )
    pay[PAY_ROWS - 8:PAY_ROWS] = jnp.zeros((8, 128), F32)
    for a in range(PAIRS):
        x = scaled(skel_ref[:, a * 128:(a + 1) * 128])
        tpay[a * 8:(a + 1) * 8] = forms(x)[0]
        for c in range(3):
            row = COEF_ROWS + c * PAIRS + a
            pay[row:row + 1] = x[c:c + 1]

    lows = (0, LEAVES // 4 * RANK)
    sizes = (LEAVES // 4 * RANK, PAY_ROWS - LEAVES // 4 * RANK)

    def lid(yy, zz):
        return lax.rem(yy + 4, 4) * 4 + lax.rem(zz + 4, 4)

    def near_id(h, stage, step):
        return lid(y, z + step) if (h == 0) == (stage == 0) else lid(y + step, z)

    def block_id(h, first, second):
        return lid(y + second, z + first) if h == 0 else lid(y + first, z + second)

    stage1 = {}
    stage2 = {}

    def begin(h):
        rows = pl.ds(lows[h], sizes[h])
        for step in (1, -1):
            stage1[h, step] = remote(
                pay.at[rows], g_ref.at[leaf, rows], (near_id(h, 0, step), p)
            )

    def spread(h, first):
        rows = pl.ds(lows[h], sizes[h])
        blk = near_id(h, 0, first)
        src = pay.at[rows] if first == 0 else g_ref.at[blk, rows]
        for step in (1, -1):
            stage2[h, first, step] = remote(
                src, g_ref.at[blk, rows], (near_id(h, 1, step), p)
            )

    def forward(h, stage, blk_minus, blk_plus, got_minus, got_plus):
        part = sizes[h] // 16 * 8
        got_minus.wait_recv()
        rows = pl.ds(lows[h], part)
        one = remote(g_ref.at[blk_minus, rows], g_ref.at[blk_minus, rows], (near_id(h, stage, 1), p))
        got_plus.wait_recv()
        rows = pl.ds(lows[h] + part, sizes[h] - part)
        two = remote(g_ref.at[blk_plus, rows], g_ref.at[blk_plus, rows], (near_id(h, stage, -1), p))
        return one, two

    level = [
        dot3(base_ref[n], vec_ref[:, n * LEAF:(n + 1) * LEAF], NT) for n in range(LEAVES)
    ]
    base = 0
    row = 0
    while len(level) > 1:
        if row < COEF_ROWS:
            for g in range(len(level) // 4):
                pay[row:row + RANK] = jnp.concatenate(level[4 * g:4 * g + 4], axis=1)
                row += RANK
        if row == sizes[0]:
            pl.semaphore_wait(barrier, LEAFS + PTS)
            begin(0)
            spread(0, 0)
        if row == COEF_ROWS and len(level) == 4:
            begin(1)
            spread(1, 0)
        level = [
            dot3(
                pair_matrix(lt_ref, base + i),
                jnp.concatenate([level[2 * i], level[2 * i + 1]], axis=0),
                NN,
            )
            for i in range(len(level) // 2)
        ]
        base += len(level)
    root = level[0].T
    xs[0] = root
    upward = {0: remote(xs.at[0], xr.at[0], (leaf, p ^ 1))}

    h0 = remote(halo_src.at[0], halo_dst.at[1], prv_dev)
    h1 = remote(halo_src.at[1], halo_dst.at[0], nxt_dev)
    arrivals = []
    for k in range(1, PTS):
        arrivals.append(remote(tpay, tp_ref.at[p], (leaf, p ^ k)))
        arrivals.append(remote(tc_ref, tcg_ref.at[p], (leaf, p ^ k)))
    for k in range(1, LEAFS):
        arrivals.append(remote(sc_ref, scg_ref.at[leaf], (leaf ^ k, p)))
    local(tpay, tp_ref.at[p])
    local(tc_ref, tcg_ref.at[p])
    local(sc_ref, scg_ref.at[leaf])

    local(pay, g_ref.at[leaf])

    r16 = lax.broadcasted_iota(jnp.int32, (16, UPN), 0)
    c16 = lax.broadcasted_iota(jnp.int32, (16, UPN), 1)
    pick = jnp.zeros((16, UPN), F32)
    for u in range(UPPER):
        first = up_offset(u) + lax.shift_right_logical(me, u + 1) * 2
        pick = jnp.where(jnp.logical_and(r16 // 2 == u, c16 == first + (r16 & 1)), 1.0, pick)
    pick = pick.astype(BF16)
    locals_[0].wait()

    @pl.loop(0, RANK // 2)
    def _(r):
        h, l = split(up_all[pl.ds(pl.multiple_of(r * 128, 128), 128), :])
        got = dg(pick, h, NT) + dg(pick, l, NT)
        ut[pl.ds(2 * r, 16, stride=RANK), :] = got[:, :RANK]
        ut[pl.ds(2 * r + 1, 16, stride=RANK), :] = got[:, RANK:]

    def upper(u, k):
        return ut[(2 * u + k) * RANK:(2 * u + k + 1) * RANK, :]

    opposite = {}

    def step_a():
        for h in range(2):
            opposite[h] = forward(
                h, 0, near_id(h, 0, -1), near_id(h, 0, 1), stage1[h, 1], stage1[h, -1]
            )
            spread(h, -1)
            spread(h, 1)

    def step_b():
        for h in range(2):
            opposite[h][0].wait_recv()
            opposite[h][1].wait_recv()
            spread(h, 2)

    last = []

    def step_c(first):
        for h in range(2):
            last.extend(
                forward(
                    h, 1, block_id(h, first, -1), block_id(h, first, 1),
                    stage2[h, first, 1], stage2[h, first, -1],
                )
            )

    def send_up(u, value):
        xs[u] = value
        dev = (leaf, p ^ (1 << u)) if u < 3 else (leaf ^ (1 << (u - 3)), p)
        upward[u] = remote(xs.at[u], xr.at[u], dev)

    def climb(u):
        upward[u].wait_recv()
        node = lax.shift_right_logical(me, u)
        left_side = lax.rem(node, 2) == 0
        own = xs[u]
        sib = xr[u]
        pair = jnp.concatenate(
            [jnp.where(left_side, own, sib), jnp.where(left_side, sib, own)], axis=1
        )
        if u < UPPER - 1:
            mat = jnp.concatenate([upper(u, 0), upper(u, 1)], axis=1)
            send_up(u + 1, dot3(pair, mat, NT))
        col = pl.multiple_of((up_offset(u) + (node // 2) * 2) * RANK, 128)
        u8, w8 = forms(scaled(upp_ref[:, pl.ds(col, 128)]))
        kern = matern(dg(stack_u(u8).T.astype(BF16), stack_w(w8).astype(BF16), NN))
        lane_left = lax.broadcasted_iota(jnp.int32, (VEC, 2 * RANK), 1) < RANK
        only_sib = jnp.where(jnp.logical_xor(lane_left, left_side), pair, 0.0)
        out = dot3(only_sib, kern, NN)
        sf[u] = jnp.where(left_side, out[:, :RANK], out[:, RANK:])

    def prepare(slot, vec, pts):
        vh, vl = split(vec)
        lanes = pl.ds(pl.multiple_of(slot * LEAF, LEAF), LEAF)
        v_scr[0:VEC, lanes] = vh
        v_scr[VEC:2 * VEC, lanes] = vl
        u8, w8 = forms(scaled(pts))
        w_scr[:, lanes] = stack_w(w8).astype(BF16)
        u_scr[lanes, :] = stack_u(u8).T.astype(BF16)

    @pl.loop(0, LEAVES)
    def _(m):
        lanes = pl.ds(pl.multiple_of(m * LEAF, LEAF), LEAF)
        prepare(m + 1, vec_ref[:, lanes], pts_ref[:, lanes])

    def near(m):
        lanes = pl.ds(pl.multiple_of(m * LEAF, LEAF), LEAF)
        w = w_scr[:, lanes]
        total = None
        for b in range(3):
            src = pl.ds(pl.multiple_of((m - 1 + b) * LEAF, LEAF), LEAF)
            kh, kl = split(matern(dg(u_scr[src, :], w, NN)))
            v = v_scr[:, src]
            big = dg(v, kh, NN)
            part = big[:VEC] + (big[VEC:] + dg(v[:VEC], kl, NN))
            total = part if total is None else total + part
        near_ref[:, pl.ds(pl.multiple_of((m - 1) * LEAF, LEAF), LEAF)] = total

    def near_span(lo, hi):
        @pl.loop(lo, hi)
        def _(m):
            near(m)

    step_a()
    climb(0)
    near_span(2, 3)
    climb(1)
    near_span(3, 4)
    step_b()
    climb(2)
    near_span(4, 6)
    step_c(0)
    climb(3)
    near_span(6, 8)
    climb(4)
    near_span(8, 10)
    step_c(-1)
    climb(5)
    near_span(10, 12)
    step_c(1)
    climb(6)
    near_span(12, 14)
    step_c(2)
    near_span(14, 16)
    h0.wait_recv()
    h1.wait_recv()
    for side, slot, edge in ((0, 0, 0), (1, LEAVES + 1, 127)):
        vec = jnp.where(me == edge, 0.0, halo_dst[side, 0:VEC])
        prepare(slot, vec, halo_dst[side, VEC:VEC + 3])
    near(1)
    near(LEAVES)

    far = sf[UPPER - 1]
    for u in range(UPPER - 2, -1, -1):
        left_side = lax.rem(lax.shift_right_logical(me, u), 2) == 0
        mat = jnp.where(left_side, upper(u, 0), upper(u, 1))
        far = sf[u] + dot3(far, mat, NN)
    far_ref[...] = far

    for c in arrivals:
        c.wait_recv()
    for c in last:
        c.wait_recv()
    for c in sends:
        c.wait_send()
    for c in locals_[1:]:
        c.wait()


def couple_kernel(
    g_hbm, tp_hbm, sc_hbm, tc_hbm, o_ref, g_ref, tp_ref, sc_ref, tc_ref, sem, ct, wt, ut, masks, sums, d_scr, k_scr, acc_a, acc_b,
):
    leaf = lax.axis_index("leaf")
    p = lax.axis_index("pts")
    lane = lax.broadcasted_iota(jnp.int32, (16, 128), 1)
    low = lax.broadcasted_iota(jnp.int32, (RANK, 128), 1) < RANK

    def rows_of(index, size):
        return pl.ds(pl.multiple_of(index * size, size), size)

    blocks = [pltpu.make_async_copy(g_hbm.at[s], g_ref.at[s], sem.at[s]) for s in range(LEAFS)]
    others = [
        pltpu.make_async_copy(a, b, sem.at[LEAFS + i])
        for i, (a, b) in enumerate(((tp_hbm, tp_ref), (sc_hbm, sc_ref), (tc_hbm, tc_ref)))
    ]
    for copy in blocks + others:
        copy.start()

    for q in range(4):
        masks[q] = (lane // VEC == q).astype(F32).astype(BF16)
    for q in range(2):
        masks[4 + q] = (lane // RANK == q).astype(F32).astype(BF16)
    r = lax.broadcasted_iota(jnp.int32, (512, 128), 0)
    c = lax.broadcasted_iota(jnp.int32, (512, 128), 1)
    sums[...] = jnp.logical_and(
        lax.rem(r, VEC) == lax.rem(c, VEC), r // 128 == c // VEC
    ).astype(F32).astype(BF16)

    def masked(x, m):
        return (x.reshape(-1, 16, 128) * masks[m][None]).reshape(x.shape)

    @pl.loop(0, LEAFS)
    def _(s):
        pltpu.make_async_copy(g_hbm.at[s], g_ref.at[s], sem.at[s]).wait()
        for g in range(GROUPS):
            c = g_ref[s, g * RANK:(g + 1) * RANK, :]
            for j in range(2):
                h, l = split(pltpu.roll(c, RANK, 1) if j else c)
                rows = (s * GROUPS + g) * 2 + j
                ct[rows_of(rows, 2 * RANK), :] = jnp.concatenate([h, l], axis=0)
        for a in range(PAIRS):
            x = jnp.concatenate(
                [
                    g_ref[s, COEF_ROWS + c * PAIRS + a:COEF_ROWS + c * PAIRS + a + 1, :]
                    for c in range(3)
                ],
                axis=0,
            )
            w = forms(x)[1]
            for j in range(2):
                rows = (s * PAIRS + a) * 2 + j
                wt[rows_of(rows, DEPTH), :] = stack_w(
                    pltpu.roll(w, RANK, 1) if j else w
                ).astype(BF16)

    for copy in others:
        copy.wait()
    ut[NODES * RANK:(NODES + 1) * RANK, :] = jnp.zeros((RANK, 2 * DEPTH), BF16)
    slot_a = lax.broadcasted_iota(jnp.int32, (RANK, 2 * DEPTH), 1) < DEPTH

    @pl.loop(0, PTS)
    def _(d):
        for a in range(PAIRS):
            t = stack_u(tp_ref[d, a * 8:(a + 1) * 8, :])
            ut[2 * a * RANK:(2 * a + 2) * RANK, :] = jnp.concatenate([t, t], axis=0).T.astype(BF16)
        acc_a[...] = jnp.zeros_like(acc_a)
        acc_b[...] = jnp.zeros_like(acc_b)

        @pl.loop(0, 3)
        def _(lev):
            ids = []
            for s in range(LEAFS):
                na = s * NODES + sc_ref[s, lev * 2, leaf * PTS + d]
                nb = s * NODES + sc_ref[s, lev * 2 + 1, leaf * PTS + d]
                ra = rows_of(tc_ref[d, lev * 2, s * PTS + p], RANK)
                rb = rows_of(tc_ref[d, lev * 2 + 1, s * PTS + p], RANK)
                ids.append((na, nb, ra, rb))
            for s, (na, nb, ra, rb) in enumerate(ids):
                u = jnp.where(slot_a, ut[ra, :], ut[rb, :])
                wa = masked(wt[rows_of(na, DEPTH), :], 4)
                wb = masked(wt[rows_of(nb ^ 1, DEPTH), :], 5)
                d_scr[s * RANK:(s + 1) * RANK] = dg(u, jnp.concatenate([wa, wb], axis=0), NN)
            for s in range(LEAFS):
                h, l = split(matern(d_scr[s * RANK:(s + 1) * RANK]))
                k_scr[s * RANK:(s + 1) * RANK] = jnp.concatenate([h, l, h], axis=1)
            for s, (na, nb, ra, rb) in enumerate(ids):
                xa = masked(ct[rows_of(na >> 1, 2 * RANK), :], na & 1)
                xb = masked(ct[rows_of((nb >> 1) ^ 1, 2 * RANK), :], 2 + (nb & 1))
                high = jnp.concatenate([xa[:RANK], xb[:RANK]], axis=0)
                rest = jnp.concatenate([xa[RANK:], xb[RANK:]], axis=0)
                k = k_scr[s * RANK:(s + 1) * RANK]
                part = dg(k, jnp.concatenate([high, high, rest], axis=0), NN)
                acc_a[ra, :] += part
                acc_b[rb, :] += part

        for g in range(GROUPS):
            parts = []
            for q in range(4):
                rows = slice((4 * g + q) * RANK, (4 * g + q + 1) * RANK)
                parts.append(jnp.where(low, acc_a[rows, :], acc_b[rows, :]))
            h, l = split(jnp.concatenate(parts, axis=1))
            o_ref[d, g * RANK:(g + 1) * RANK, :] = dg(h, sums[...], NN) + dg(l, sums[...], NN)


def scatter_kernel(
    acc_hbm, far_hbm, lt_hbm, base_hbm, near_hbm, out_ref,
    acc_ref, far_ref, lt_ref, base_ref, near_ref, from_core, s1, s2, work, ssem, rsem, lsem,
):
    leaf = lax.axis_index("leaf")
    p = lax.axis_index("pts")
    x = p // 2
    core = lax.rem(p, 2)
    sister = (leaf, p ^ 1)

    own_blocks = {}
    steps = (2, 1, 3, 0)
    for st in steps:
        blk = lax.rem(x + st, 4) * 2 + core
        own_blocks[st] = pltpu.make_async_copy(acc_hbm.at[blk], acc_ref.at[st], lsem.at[st])
        own_blocks[st].start()
    others = [
        pltpu.make_async_copy(a, b, lsem.at[4 + i])
        for i, (a, b) in enumerate(
            ((far_hbm, far_ref), (lt_hbm, lt_ref), (base_hbm, base_ref), (near_hbm, near_ref))
        )
    ]
    for copy in others:
        copy.start()

    def dev(step):
        return (leaf, lax.rem(x + step + 4, 4) * 2 + core)

    barrier = pltpu.get_barrier_semaphore()
    for d in (sister, dev(1), dev(-1)):
        pl.semaphore_signal(barrier, inc=1, device_id=d, device_id_type=MESH)
    pl.semaphore_wait(barrier, 3)

    sends = []

    def remote(src, dst, device):
        i = len(sends)
        copy = pltpu.make_async_remote_copy(
            src_ref=src, dst_ref=dst, send_sem=ssem.at[i], recv_sem=rsem.at[i],
            device_id=device, device_id_type=MESH,
        )
        copy.start()
        sends.append(copy)
        return copy

    half = COEF_ROWS // 2
    first = {}
    for st in steps:
        xx = lax.rem(x + st, 4)
        first[st] = remote(acc_hbm.at[xx * 2 + 1 - core], from_core.at[st], sister)

    def summed(st):
        first[st].wait_recv()
        own_blocks[st].wait()
        return acc_ref[st] + from_core[st]

    work[0] = summed(2)
    a1 = remote(work.at[0, pl.ds(0, half)], s1.at[pl.ds(0, half)], dev(1))
    b1 = remote(work.at[0, pl.ds(half, half)], s1.at[pl.ds(half, half)], dev(-1))
    work[1] = summed(1)
    work[2] = summed(3)
    a1.wait_recv()
    work[1, 0:half] += s1[0:half]
    a2 = remote(work.at[1], s2.at[0], dev(1))
    b1.wait_recv()
    work[2, half:] += s1[half:]
    b2 = remote(work.at[2], s2.at[1], dev(-1))

    def down(node, n):
        return dot3(node, pair_matrix(lt_ref, n), NN)

    for copy in others:
        copy.wait()
    top = down(far_ref[...], 14)
    level2 = [down(top[:, :RANK], 12), down(top[:, RANK:], 13)]
    own = summed(0)
    a2.wait_recv()
    b2.wait_recv()
    work[3] = own + (s2[0] + s2[1])

    turned = [work[3, g * RANK:(g + 1) * RANK].T for g in range(GROUPS)]

    def coupling(a):
        t = turned[a // 2]
        r = (a % 2) * 2 * VEC
        return jnp.concatenate([t[r:r + VEC], t[r + VEC:r + 2 * VEC]], axis=1)

    pairs = [level2[i] + coupling(12 + i) for i in range(2)]
    pairs = [
        down(pairs[i // 2][:, (i % 2) * RANK:(i % 2 + 1) * RANK], 8 + i) + coupling(8 + i)
        for i in range(4)
    ]
    pairs = [
        down(pairs[i // 2][:, (i % 2) * RANK:(i % 2 + 1) * RANK], i) + coupling(i)
        for i in range(8)
    ]
    for m in range(LEAVES):
        c = pairs[m // 2][:, (m % 2) * RANK:(m % 2 + 1) * RANK]
        cols = slice(m * LEAF, (m + 1) * LEAF)
        out_ref[:, cols] = near_ref[:, cols] + dot3(c, base_ref[m], NN)
    for c in sends:
        c.wait_send()


def vmem():
    return pl.BlockSpec(memory_space=pltpu.VMEM)


def anywhere():
    return pl.BlockSpec(memory_space=pl.ANY)


def shape(*dims, dtype=F32):
    return jax.ShapeDtypeStruct(dims, dtype)


def on_device(
    vectors, points, leaf_bases, local_transfer, skel_points, up_transfer, up_points,
    source_ids, target_ids, live_counts,
):
    me = lax.axis_index("leaf") * PTS + lax.axis_index("pts")
    counts = jnp.array([LEAVES, LEAVES // 2, LEAVES // 4], jnp.int32)
    starts = jnp.array([0, LEAVES, LEAVES + LEAVES // 2], jnp.int32)
    shift = (starts - me * counts)[:, None, None]
    slot = jnp.arange(2, dtype=jnp.int32)
    source_code = jnp.swapaxes(source_ids[:, 0], 1, 2) + shift
    target_code = jnp.where(
        slot[None, :, None] < live_counts[:, 0, None, :],
        jnp.swapaxes(target_ids[:, 0], 1, 2) + shift,
        NODES,
    )
    source_code = jnp.pad(source_code.reshape(6, 128), ((0, 2), (0, 0)))
    target_code = jnp.pad(target_code.reshape(6, 128), ((0, 2), (0, 0)))
    lt = local_transfer[0]
    up_rows = jnp.transpose(up_transfer, (1, 2, 0)).reshape(RANK * RANK, UPN)
    n_remote = 96

    gathered, near, far, tp, scg, tcg = pl.pallas_call(
        gather_kernel,
        out_shape=(
            shape(LEAFS, PAY_ROWS, 128), shape(VEC, LEAVES * LEAF), shape(VEC, RANK),
            shape(PTS, PAIRS * 8, 128), shape(LEAFS, 8, 128, dtype=jnp.int32),
            shape(PTS, 8, 128, dtype=jnp.int32),
        ),
        in_specs=[vmem()] * 5 + [anywhere()] + [vmem()] * 3,
        out_specs=(vmem(),) * 6,
        scratch_shapes=[
            pltpu.VMEM((18 * LEAF, DEPTH), BF16),
            pltpu.VMEM((DEPTH, 18 * LEAF), BF16),
            pltpu.VMEM((2 * VEC, 18 * LEAF), BF16),
            pltpu.VMEM((2, VEC + 8, LEAF), F32),
            pltpu.VMEM((2, VEC + 8, LEAF), F32),
            pltpu.VMEM((PAY_ROWS, 128), F32),
            pltpu.VMEM((PAIRS * 8, 128), F32),
            pltpu.VMEM((RANK * RANK, UPN), F32),
            pltpu.VMEM((16 * RANK, RANK), F32),
            pltpu.VMEM((UPPER, VEC, RANK), F32),
            pltpu.VMEM((UPPER, VEC, RANK), F32),
            pltpu.VMEM((UPPER, VEC, RANK), F32),
            pltpu.SemaphoreType.DMA((n_remote,)),
            pltpu.SemaphoreType.DMA((n_remote,)),
            pltpu.SemaphoreType.DMA((16,)),
        ],
        compiler_params=pltpu.CompilerParams(
            collective_id=0, has_side_effects=True, vmem_limit_bytes=48 << 20
        ),
    )(vectors, points, leaf_bases, lt, skel_points, up_rows, up_points, source_code, target_code)

    partial = pl.pallas_call(
        couple_kernel,
        out_shape=shape(PTS, COEF_ROWS, 128),
        in_specs=[anywhere()] * 4,
        out_specs=vmem(),
        scratch_shapes=[
            pltpu.VMEM((LEAFS, PAY_ROWS, 128), F32),
            pltpu.VMEM((PTS, PAIRS * 8, 128), F32),
            pltpu.SMEM((LEAFS, 8, 128), jnp.int32),
            pltpu.SMEM((PTS, 8, 128), jnp.int32),
            pltpu.SemaphoreType.DMA((LEAFS + 3,)),
            pltpu.VMEM((LEAFS * GROUPS * 4 * RANK, 128), BF16),
            pltpu.VMEM((LEAFS * NODES * DEPTH, 128), BF16),
            pltpu.VMEM(((NODES + 1) * RANK, 2 * DEPTH), BF16),
            pltpu.VMEM((8, 16, 128), BF16),
            pltpu.VMEM((512, 128), BF16),
            pltpu.VMEM((LEAFS * RANK, 128), F32),
            pltpu.VMEM((LEAFS * RANK, 3 * 128), BF16),
            pltpu.VMEM(((NODES + 1) * RANK, 128), F32),
            pltpu.VMEM(((NODES + 1) * RANK, 128), F32),
        ],
        compiler_params=pltpu.CompilerParams(vmem_limit_bytes=56 << 20),
    )(gathered, tp, scg, tcg)

    return pl.pallas_call(
        scatter_kernel,
        out_shape=shape(VEC, LEAVES * LEAF),
        in_specs=[anywhere()] * 5,
        out_specs=vmem(),
        scratch_shapes=[
            pltpu.VMEM((4, COEF_ROWS, 128), F32),
            pltpu.VMEM((VEC, RANK), F32),
            pltpu.VMEM((30, RANK, RANK), F32),
            pltpu.VMEM((LEAVES, RANK, LEAF), F32),
            pltpu.VMEM((VEC, LEAVES * LEAF), F32),
            pltpu.VMEM((4, COEF_ROWS, 128), F32),
            pltpu.VMEM((COEF_ROWS, 128), F32),
            pltpu.VMEM((2, COEF_ROWS, 128), F32),
            pltpu.VMEM((4, COEF_ROWS, 128), F32),
            pltpu.SemaphoreType.DMA((8,)),
            pltpu.SemaphoreType.DMA((8,)),
            pltpu.SemaphoreType.DMA((8,)),
        ],
        compiler_params=pltpu.CompilerParams(
            collective_id=1, has_side_effects=True, vmem_limit_bytes=48 << 20
        ),
    )(partial, far, lt, leaf_bases, near)


def solution(mesh):
    both = ("leaf", "pts")
    return jax.shard_map(
        on_device,
        mesh=mesh,
        in_specs=(
            P(None, both),
            P(None, both),
            P(both, None, None),
            P(both, None, None, None),
            P(None, both),
            P(),
            P(),
            P(None, both, None, None),
            P(None, both, None, None),
            P(None, both, None),
        ),
        out_specs=P(None, both),
        check_vma=False,
    )
```

```python
import functools
import math

import jax
import jax.numpy as jnp
from jax import lax
from jax.experimental import pallas as pl
from jax.experimental.pallas import tpu as pltpu
from jax.sharding import PartitionSpec as P

F32 = jnp.float32
BF16 = jnp.bfloat16
MESH = pl.DeviceIdType.MESH
LN2 = math.log(2.0)
KAPPA = math.sqrt(3.0) / 0.3 / LN2
TINY = 1e-30

VEC = 32
RANK = 64
LEAF = 256
LEAVES = 16
PTS = 8
LEAFS = 16
PAIRS = 14
NODES = 28
COEF_ROWS = PAIRS * VEC
PAY_ROWS = COEF_ROWS + 48
UPPER = 7
UPN = 254
TREE = (0, 8, 12, 14, 30, 38, 42, 44)
GROUPS = NODES // 4
DEPTH = 48
NN = (((1,), (0,)), ((), ()))
NT = (((1,), (1,)), ((), ()))


def dg(a, b, dims):
    return lax.dot_general(a, b, dims, preferred_element_type=F32)


def split(x):
    hi = x.astype(BF16)
    return hi, (x - hi.astype(F32)).astype(BF16)


def dot3(a, b, dims):
    ah, al = split(a)
    bh, bl = split(b)
    return dg(ah, bh, dims) + (dg(ah, bl, dims) + dg(al, bh, dims))


def split3(x):
    h = x.astype(BF16).astype(F32)
    r = x - h
    m = r.astype(BF16).astype(F32)
    return h, m, r - m


def scaled(pts):
    return (pts - 0.5) * KAPPA


def forms(x):
    n = x.shape[1]
    x = jnp.concatenate([x, jnp.zeros((5, n), F32)], axis=0)
    q = jnp.sum(x * x, axis=0, keepdims=True)
    row = lax.broadcasted_iota(jnp.int32, (8, n), 0)
    w = jnp.where(row < 3, x, jnp.where(row == 3, 1.0, jnp.where(row == 4, q, 0.0)))
    u = jnp.where(row < 3, -2.0 * x, jnp.where(row == 3, q, jnp.where(row == 4, 1.0, 0.0)))
    return u, w


def stack_u(u):
    h, m, l = split3(u)
    return jnp.concatenate([h, h, m, m, h, l], axis=0)


def stack_w(w):
    h, m, l = split3(w)
    return jnp.concatenate([h, m, h, m, l, h], axis=0)


def matern(squared):
    squared = jnp.maximum(squared, TINY)
    t = squared * lax.rsqrt(squared)
    return (1.0 + LN2 * t) * jnp.exp2(-t)


def pair_matrix(lt_ref, n):
    return jnp.concatenate([lt_ref[2 * n], lt_ref[2 * n + 1]], axis=1)


def up_offset(u):
    return 0 if u == 0 else 256 - (128 >> (u - 1))


def gather_kernel(
    vec_hbm, pts_hbm, base_hbm, lt_hbm, skel_hbm, upt_ref, upp_hbm, src_ref, tgt_ref, live_ref,
    g_ref, near_ref, far_ref, tp_ref, scg_ref, tcg_ref,
    vec_ref, pts_ref, base_ref, lt_ref, skel_ref, upp_ref, sc_ref, tc_ref, u_scr, w_scr, v_scr, halo_src, halo_dst, pay, tpay, up_all, ut, tree, sf,
    ssem, rsem, lsem,
):
    leaf = lax.axis_index("leaf")
    p = lax.axis_index("pts")
    me = leaf * PTS + p
    y = leaf // 4
    z = lax.rem(leaf, 4)
    nxt = lax.rem(me + 1, 128)
    prv = lax.rem(me + 127, 128)
    nxt_dev = (nxt // PTS, lax.rem(nxt, PTS))
    prv_dev = (prv // PTS, lax.rem(prv, PTS))

    barrier = pltpu.get_barrier_semaphore()
    for k in range(1, LEAFS):
        pl.semaphore_signal(barrier, inc=1, device_id=(leaf ^ k, p), device_id_type=MESH)
    for k in range(1, PTS):
        pl.semaphore_signal(barrier, inc=1, device_id=(leaf, p ^ k), device_id_type=MESH)
    pl.semaphore_signal(barrier, inc=1, device_id=nxt_dev, device_id_type=MESH)
    pl.semaphore_signal(barrier, inc=1, device_id=prv_dev, device_id_type=MESH)

    counter = [0]
    sends = []

    def remote(src, dst, dev):
        i = counter[0]
        counter[0] += 1
        copy = pltpu.make_async_remote_copy(
            src_ref=src, dst_ref=dst, send_sem=ssem.at[i], recv_sem=rsem.at[i],
            device_id=dev, device_id_type=MESH,
        )
        copy.start()
        sends.append(copy)
        return copy

    locals_ = []

    def local(src, dst):
        copy = pltpu.make_async_copy(src, dst, lsem.at[len(locals_)])
        copy.start()
        locals_.append(copy)

    for src, dst in (
        (skel_hbm, skel_ref), (vec_hbm, vec_ref), (base_hbm, base_ref), (lt_hbm, lt_ref),
        (pts_hbm, pts_ref), (upp_hbm, upp_ref), (upt_ref, up_all),
    ):
        local(src, dst)

    sc_ref[...] = jnp.zeros_like(sc_ref)
    tc_ref[...] = jnp.zeros_like(tc_ref)
    for lev in range(3):
        shift = LEAVES * 2 - (LEAVES * 2 >> lev) - me * (LEAVES >> lev)
        for k in range(2):
            row = slice(2 * lev + k, 2 * lev + k + 1)
            sc_ref[row] = src_ref[lev, k:k + 1] + shift
            tc_ref[row] = jnp.where(k < live_ref[lev], tgt_ref[lev, k:k + 1] + shift, NODES)

    locals_[0].wait()
    pay[PAY_ROWS - 8:PAY_ROWS] = jnp.zeros((8, 128), F32)
    for a in range(PAIRS):
        x = scaled(skel_ref[:, a * 128:(a + 1) * 128])
        tpay[a * 8:(a + 1) * 8] = forms(x)[0]
        for c in range(3):
            row = COEF_ROWS + c * PAIRS + a
            pay[row:row + 1] = x[c:c + 1]

    lows = (0, LEAVES // 4 * RANK)
    sizes = (LEAVES // 4 * RANK, PAY_ROWS - LEAVES // 4 * RANK)

    def lid(yy, zz):
        return lax.rem(yy + 4, 4) * 4 + lax.rem(zz + 4, 4)

    def near_id(h, stage, step):
        return lid(y, z + step) if (h == 0) == (stage == 0) else lid(y + step, z)

    def block_id(h, first, second):
        return lid(y + second, z + first) if h == 0 else lid(y + first, z + second)

    stage1 = {}
    stage2 = {}

    def begin(h):
        rows = pl.ds(lows[h], sizes[h])
        for step in (1, -1):
            stage1[h, step] = remote(
                pay.at[rows], g_ref.at[leaf, rows], (near_id(h, 0, step), p)
            )

    def spread(h, first):
        rows = pl.ds(lows[h], sizes[h])
        blk = near_id(h, 0, first)
        src = pay.at[rows] if first == 0 else g_ref.at[blk, rows]
        for step in (1, -1):
            stage2[h, first, step] = remote(
                src, g_ref.at[blk, rows], (near_id(h, 1, step), p)
            )

    def forward(h, stage, blk_minus, blk_plus, got_minus, got_plus):
        part = sizes[h] // 16 * 8
        got_minus.wait_recv()
        rows = pl.ds(lows[h], part)
        one = remote(g_ref.at[blk_minus, rows], g_ref.at[blk_minus, rows], (near_id(h, stage, 1), p))
        got_plus.wait_recv()
        rows = pl.ds(lows[h] + part, sizes[h] - part)
        two = remote(g_ref.at[blk_plus, rows], g_ref.at[blk_plus, rows], (near_id(h, stage, -1), p))
        return one, two

    for i in (1, 2, 3):
        locals_[i].wait()
    level = [
        dot3(base_ref[n], vec_ref[:, n * LEAF:(n + 1) * LEAF], NT) for n in range(LEAVES)
    ]
    base = 0
    row = 0
    while len(level) > 1:
        if row < COEF_ROWS:
            for g in range(len(level) // 4):
                pay[row:row + RANK] = jnp.concatenate(level[4 * g:4 * g + 4], axis=1)
                row += RANK
        if row == sizes[0]:
            pl.semaphore_wait(barrier, LEAFS + PTS)
            begin(0)
            spread(0, 0)
        if row == COEF_ROWS and len(level) == 4:
            begin(1)
            spread(1, 0)
        level = [
            dot3(
                pair_matrix(lt_ref, base + i),
                jnp.concatenate([level[2 * i], level[2 * i + 1]], axis=0),
                NN,
            )
            for i in range(len(level) // 2)
        ]
        base += len(level)
    root = level[0].T
    tree[p] = root
    roots = [remote(tree.at[p], tree.at[p], (leaf, p ^ k)) for k in range(1, PTS)]

    for i in (4, 5):
        locals_[i].wait()
    for side, off in ((0, 0), (1, (LEAVES - 1) * LEAF)):
        halo_src[side, 0:VEC] = vec_ref[:, off:off + LEAF]
        halo_src[side, VEC:VEC + 8] = jnp.concatenate(
            [pts_ref[:, off:off + LEAF], jnp.zeros((5, LEAF), F32)], axis=0
        )
    h0 = remote(halo_src.at[0], halo_dst.at[1], prv_dev)
    h1 = remote(halo_src.at[1], halo_dst.at[0], nxt_dev)
    arrivals = []
    for k in range(1, PTS):
        arrivals.append(remote(tpay, tp_ref.at[p], (leaf, p ^ k)))
        arrivals.append(remote(tc_ref, tcg_ref.at[p], (leaf, p ^ k)))
    for k in range(1, LEAFS):
        arrivals.append(remote(sc_ref, scg_ref.at[leaf], (leaf ^ k, p)))
    local(tpay, tp_ref.at[p])
    local(tc_ref, tcg_ref.at[p])
    local(sc_ref, scg_ref.at[leaf])

    local(pay, g_ref.at[leaf])

    r48 = lax.broadcasted_iota(jnp.int32, (48, UPN), 0)
    c48 = lax.broadcasted_iota(jnp.int32, (48, UPN), 1)
    want = jnp.where(
        r48 < 8, leaf * 8 + r48,
        jnp.where(r48 < 12, 120 + leaf * 4 + r48, jnp.where(r48 < 14, 180 + leaf * 2 + r48, 210 + r48)),
    )
    pick = (c48 == want).astype(F32).astype(BF16)

    def pick_rows(lo, hi):
        @pl.loop(lo, hi)
        def _(r):
            halves = [
                split(up_all[pl.ds(pl.multiple_of(r * 512 + i * 128, 128), 128), :])
                for i in range(4)
            ]
            got = [dg(pick, h, NT) + dg(pick, l, NT) for h, l in halves]
            for i, x in enumerate(got):
                ut[pl.ds(8 * r + 2 * i, 48, stride=RANK), :] = x[:, :RANK]
                ut[pl.ds(8 * r + 2 * i + 1, 48, stride=RANK), :] = x[:, RANK:]

    opposite = {}

    def step_a():
        for h in range(2):
            opposite[h] = forward(
                h, 0, near_id(h, 0, -1), near_id(h, 0, 1), stage1[h, 1], stage1[h, -1]
            )
            spread(h, -1)
            spread(h, 1)

    def step_b():
        for h in range(2):
            opposite[h][0].wait_recv()
            opposite[h][1].wait_recv()
            spread(h, 2)

    last = []

    def step_c(first):
        for h in range(2):
            last.extend(
                forward(
                    h, 1, block_id(h, first, -1), block_id(h, first, 1),
                    stage2[h, first, 1], stage2[h, first, -1],
                )
            )

    def matrix(n):
        return ut[pl.ds(pl.multiple_of(n * RANK, RANK), RANK), :]

    def parent(n):
        return dot3(
            jnp.concatenate([tree[n], tree[n + 1]], axis=1),
            jnp.concatenate([matrix(n), matrix(n + 1)], axis=1),
            NT,
        )

    def raise_level(u):
        return [parent(TREE[u] + 2 * i) for i in range((TREE[u + 1] - TREE[u]) // 2)]

    def own_node(u):
        return p >> u if u < 3 else leaf >> (u - 3)

    def lower_levels():
        for c in roots:
            c.wait_recv()
        for u in range(2):
            for i, x in enumerate(raise_level(u)):
                tree[TREE[u + 1] + i] = x
        mine = TREE[3] + leaf
        tree[mine] = raise_level(2)[0]
        return [remote(tree.at[mine], tree.at[mine], (leaf ^ k, p)) for k in range(1, LEAFS)]

    def upper_levels(tops):
        for c in tops:
            c.wait_recv()
        for u in range(3, 6):
            for i, x in enumerate(raise_level(u)):
                tree[TREE[u + 1] + i] = x

    def sibling_fields():
        lane_left = lax.broadcasted_iota(jnp.int32, (VEC, 2 * RANK), 1) < RANK
        distances = []
        for u in range(UPPER):
            first = lax.shift_right_logical(me, u + 1) * 2
            col = pl.multiple_of((up_offset(u) + first) * RANK, 128)
            u8, w8 = forms(scaled(upp_ref[:, pl.ds(col, 128)]))
            distances.append(dg(stack_u(u8).T.astype(BF16), stack_w(w8).astype(BF16), NN))
        kernels = [matern(x) for x in distances]
        for u in range(UPPER):
            left_side = lax.rem(own_node(u), 2) == 0
            sib = tree[TREE[u] + (own_node(u) ^ 1)]
            pair = jnp.concatenate([sib, sib], axis=1)
            only_sib = jnp.where(jnp.logical_xor(lane_left, left_side), pair, 0.0)
            out = dot3(only_sib, kernels[u], NN)
            sf[u] = jnp.where(left_side, out[:, :RANK], out[:, RANK:])

    def prepare(slot, vec, pts):
        vh, vl = split(vec)
        lanes = pl.ds(pl.multiple_of(slot * LEAF, LEAF), LEAF)
        v_scr[0:VEC, lanes] = vh
        v_scr[VEC:2 * VEC, lanes] = vl
        u8, w8 = forms(scaled(pts))
        w_scr[:, lanes] = stack_w(w8).astype(BF16)
        u_scr[lanes, :] = stack_u(u8).T.astype(BF16)

    def near(m):
        lanes = pl.ds(pl.multiple_of(m * LEAF, LEAF), LEAF)
        w = w_scr[:, lanes]
        total = None
        for b in range(3):
            src = pl.ds(pl.multiple_of((m - 1 + b) * LEAF, LEAF), LEAF)
            kh, kl = split(matern(dg(u_scr[src, :], w, NN)))
            v = v_scr[:, src]
            big = dg(v, kh, NN)
            part = big[:VEC] + (big[VEC:] + dg(v[:VEC], kl, NN))
            total = part if total is None else total + part
        near_ref[:, pl.ds(pl.multiple_of((m - 1) * LEAF, LEAF), LEAF)] = total

    def near_span(lo, hi):
        @pl.loop(lo, hi)
        def _(m):
            near(m)

    step_a()
    locals_[6].wait()
    pick_rows(0, 4)
    step_b()
    pick_rows(4, 8)
    tops = lower_levels()
    step_c(0)

    @pl.loop(0, LEAVES)
    def _(m):
        lanes = pl.ds(pl.multiple_of(m * LEAF, LEAF), LEAF)
        prepare(m + 1, vec_ref[:, lanes], pts_ref[:, lanes])

    near_span(2, 6)
    step_c(-1)
    near_span(6, 10)
    step_c(1)
    near_span(10, 12)
    upper_levels(tops)
    step_c(2)
    near_span(12, 16)
    sibling_fields()
    h0.wait_recv()
    h1.wait_recv()
    for side, slot, edge in ((0, 0, 0), (1, LEAVES + 1, 127)):
        vec = jnp.where(me == edge, 0.0, halo_dst[side, 0:VEC])
        prepare(slot, vec, halo_dst[side, VEC:VEC + 3])
    near(1)
    near(LEAVES)

    far = sf[UPPER - 1]
    for u in range(UPPER - 2, -1, -1):
        far = sf[u] + dot3(far, matrix(TREE[u] + own_node(u)), NN)
    far_ref[...] = far

    for c in arrivals:
        c.wait_recv()
    for c in last:
        c.wait_recv()
    for c in sends:
        c.wait_send()
    for c in locals_[7:]:
        c.wait()


def couple_kernel(
    g_hbm, tp_hbm, sc_hbm, tc_hbm, o_ref, g_ref, tp_ref, sc_ref, tc_ref, sem, ct, wt, ut, masks, sums, d_scr, k_scr, acc_a, acc_b,
):
    leaf = lax.axis_index("leaf")
    p = lax.axis_index("pts")
    lane = lax.broadcasted_iota(jnp.int32, (16, 128), 1)
    low = lax.broadcasted_iota(jnp.int32, (RANK, 128), 1) < RANK

    def rows_of(index, size):
        return pl.ds(pl.multiple_of(index * size, size), size)

    blocks = [pltpu.make_async_copy(g_hbm.at[s], g_ref.at[s], sem.at[s]) for s in range(LEAFS)]
    others = [
        pltpu.make_async_copy(a, b, sem.at[LEAFS + i])
        for i, (a, b) in enumerate(((tp_hbm, tp_ref), (sc_hbm, sc_ref), (tc_hbm, tc_ref)))
    ]
    for copy in blocks + others:
        copy.start()

    for q in range(4):
        masks[q] = (lane // VEC == q).astype(F32).astype(BF16)
    for q in range(2):
        masks[4 + q] = (lane // RANK == q).astype(F32).astype(BF16)
    r = lax.broadcasted_iota(jnp.int32, (512, 128), 0)
    c = lax.broadcasted_iota(jnp.int32, (512, 128), 1)
    sums[...] = jnp.logical_and(
        lax.rem(r, VEC) == lax.rem(c, VEC), r // 128 == c // VEC
    ).astype(F32).astype(BF16)

    def masked(x, m):
        return (x.reshape(-1, 16, 128) * masks[m][None]).reshape(x.shape)

    @pl.loop(0, LEAFS)
    def _(s):
        pltpu.make_async_copy(g_hbm.at[s], g_ref.at[s], sem.at[s]).wait()
        for g in range(GROUPS):
            c = g_ref[s, g * RANK:(g + 1) * RANK, :]
            for j in range(2):
                h, l = split(pltpu.roll(c, RANK, 1) if j else c)
                rows = (s * GROUPS + g) * 2 + j
                ct[rows_of(rows, 2 * RANK), :] = jnp.concatenate([h, l], axis=0)
        for a in range(PAIRS):
            x = jnp.concatenate(
                [
                    g_ref[s, COEF_ROWS + c * PAIRS + a:COEF_ROWS + c * PAIRS + a + 1, :]
                    for c in range(3)
                ],
                axis=0,
            )
            w = forms(x)[1]
            for j in range(2):
                rows = (s * PAIRS + a) * 2 + j
                wt[rows_of(rows, DEPTH), :] = stack_w(
                    pltpu.roll(w, RANK, 1) if j else w
                ).astype(BF16)

    for copy in others:
        copy.wait()
    ut[NODES * RANK:(NODES + 1) * RANK, :] = jnp.zeros((RANK, 2 * DEPTH), BF16)
    slot_a = lax.broadcasted_iota(jnp.int32, (RANK, 2 * DEPTH), 1) < DEPTH

    @pl.loop(0, PTS)
    def _(d):
        for a in range(PAIRS):
            t = stack_u(tp_ref[d, a * 8:(a + 1) * 8, :])
            ut[2 * a * RANK:(2 * a + 2) * RANK, :] = jnp.concatenate([t, t], axis=0).T.astype(BF16)
        acc_a[...] = jnp.zeros_like(acc_a)
        acc_b[...] = jnp.zeros_like(acc_b)

        @pl.loop(0, 3)
        def _(lev):
            ids = []
            for s in range(LEAFS):
                na = s * NODES + sc_ref[s, lev * 2, leaf * PTS + d]
                nb = s * NODES + sc_ref[s, lev * 2 + 1, leaf * PTS + d]
                ra = rows_of(tc_ref[d, lev * 2, s * PTS + p], RANK)
                rb = rows_of(tc_ref[d, lev * 2 + 1, s * PTS + p], RANK)
                ids.append((na, nb, ra, rb))
            for s, (na, nb, ra, rb) in enumerate(ids):
                u = jnp.where(slot_a, ut[ra, :], ut[rb, :])
                wa = masked(wt[rows_of(na, DEPTH), :], 4)
                wb = masked(wt[rows_of(nb ^ 1, DEPTH), :], 5)
                d_scr[s * RANK:(s + 1) * RANK] = dg(u, jnp.concatenate([wa, wb], axis=0), NN)
            for s in range(LEAFS):
                h, l = split(matern(d_scr[s * RANK:(s + 1) * RANK]))
                k_scr[s * RANK:(s + 1) * RANK] = jnp.concatenate([h, l, h], axis=1)
            for s, (na, nb, ra, rb) in enumerate(ids):
                xa = masked(ct[rows_of(na >> 1, 2 * RANK), :], na & 1)
                xb = masked(ct[rows_of((nb >> 1) ^ 1, 2 * RANK), :], 2 + (nb & 1))
                high = jnp.concatenate([xa[:RANK], xb[:RANK]], axis=0)
                rest = jnp.concatenate([xa[RANK:], xb[RANK:]], axis=0)
                k = k_scr[s * RANK:(s + 1) * RANK]
                part = dg(k, jnp.concatenate([high, high, rest], axis=0), NN)
                acc_a[ra, :] += part
                acc_b[rb, :] += part

        for g in range(GROUPS):
            parts = []
            for q in range(4):
                rows = slice((4 * g + q) * RANK, (4 * g + q + 1) * RANK)
                parts.append(jnp.where(low, acc_a[rows, :], acc_b[rows, :]))
            h, l = split(jnp.concatenate(parts, axis=1))
            o_ref[d, g * RANK:(g + 1) * RANK, :] = dg(h, sums[...], NN) + dg(l, sums[...], NN)


def scatter_kernel(
    acc_hbm, far_hbm, lt_hbm, base_hbm, near_hbm, out_ref,
    acc_ref, far_ref, lt_ref, base_ref, near_ref, from_core, s1, s2, work, ssem, rsem, lsem,
):
    leaf = lax.axis_index("leaf")
    p = lax.axis_index("pts")
    x = p // 2
    core = lax.rem(p, 2)
    sister = (leaf, p ^ 1)

    own_blocks = {}
    steps = (2, 1, 3, 0)
    for st in steps:
        blk = lax.rem(x + st, 4) * 2 + core
        own_blocks[st] = pltpu.make_async_copy(acc_hbm.at[blk], acc_ref.at[st], lsem.at[st])
        own_blocks[st].start()
    others = [
        pltpu.make_async_copy(a, b, lsem.at[4 + i])
        for i, (a, b) in enumerate(
            ((far_hbm, far_ref), (lt_hbm, lt_ref), (base_hbm, base_ref), (near_hbm, near_ref))
        )
    ]
    for copy in others:
        copy.start()

    def dev(step):
        return (leaf, lax.rem(x + step + 4, 4) * 2 + core)

    barrier = pltpu.get_barrier_semaphore()
    for d in (sister, dev(1), dev(-1)):
        pl.semaphore_signal(barrier, inc=1, device_id=d, device_id_type=MESH)
    pl.semaphore_wait(barrier, 3)

    sends = []

    def remote(src, dst, device):
        i = len(sends)
        copy = pltpu.make_async_remote_copy(
            src_ref=src, dst_ref=dst, send_sem=ssem.at[i], recv_sem=rsem.at[i],
            device_id=device, device_id_type=MESH,
        )
        copy.start()
        sends.append(copy)
        return copy

    half = COEF_ROWS // 2
    first = {}
    for st in steps:
        xx = lax.rem(x + st, 4)
        first[st] = remote(acc_hbm.at[xx * 2 + 1 - core], from_core.at[st], sister)

    def summed(st):
        first[st].wait_recv()
        own_blocks[st].wait()
        return acc_ref[st] + from_core[st]

    work[0] = summed(2)
    a1 = remote(work.at[0, pl.ds(0, half)], s1.at[pl.ds(0, half)], dev(1))
    b1 = remote(work.at[0, pl.ds(half, half)], s1.at[pl.ds(half, half)], dev(-1))
    work[1] = summed(1)
    work[2] = summed(3)
    a1.wait_recv()
    work[1, 0:half] += s1[0:half]
    a2 = remote(work.at[1], s2.at[0], dev(1))
    b1.wait_recv()
    work[2, half:] += s1[half:]
    b2 = remote(work.at[2], s2.at[1], dev(-1))

    def down(node, n):
        return dot3(node, pair_matrix(lt_ref, n), NN)

    for copy in others:
        copy.wait()
    top = down(far_ref[...], 14)
    level2 = [down(top[:, :RANK], 12), down(top[:, RANK:], 13)]
    own = summed(0)
    a2.wait_recv()
    b2.wait_recv()
    work[3] = own + (s2[0] + s2[1])

    turned = [work[3, g * RANK:(g + 1) * RANK].T for g in range(GROUPS)]

    def coupling(a):
        t = turned[a // 2]
        r = (a % 2) * 2 * VEC
        return jnp.concatenate([t[r:r + VEC], t[r + VEC:r + 2 * VEC]], axis=1)

    pairs = [level2[i] + coupling(12 + i) for i in range(2)]
    pairs = [
        down(pairs[i // 2][:, (i % 2) * RANK:(i % 2 + 1) * RANK], 8 + i) + coupling(8 + i)
        for i in range(4)
    ]
    pairs = [
        down(pairs[i // 2][:, (i % 2) * RANK:(i % 2 + 1) * RANK], i) + coupling(i)
        for i in range(8)
    ]
    for m in range(LEAVES):
        c = pairs[m // 2][:, (m % 2) * RANK:(m % 2 + 1) * RANK]
        cols = slice(m * LEAF, (m + 1) * LEAF)
        out_ref[:, cols] = near_ref[:, cols] + dot3(c, base_ref[m], NN)
    for c in sends:
        c.wait_send()


def vmem():
    return pl.BlockSpec(memory_space=pltpu.VMEM)


def anywhere():
    return pl.BlockSpec(memory_space=pl.ANY)


def shape(*dims, dtype=F32):
    return jax.ShapeDtypeStruct(dims, dtype)


def on_device(
    vectors, points, leaf_bases, local_transfer, skel_points, up_transfer, up_points,
    source_ids, target_ids, live_counts,
):
    sources = jnp.swapaxes(source_ids[:, 0], 1, 2)
    targets = jnp.swapaxes(target_ids[:, 0], 1, 2)
    lt = local_transfer[0]
    up_rows = jnp.transpose(up_transfer, (1, 2, 0)).reshape(RANK * RANK, UPN)
    n_remote = 112

    gathered, near, far, tp, scg, tcg = pl.pallas_call(
        gather_kernel,
        out_shape=(
            shape(LEAFS, PAY_ROWS, 128), shape(VEC, LEAVES * LEAF), shape(VEC, RANK),
            shape(PTS, PAIRS * 8, 128), shape(LEAFS, 8, 128, dtype=jnp.int32),
            shape(PTS, 8, 128, dtype=jnp.int32),
        ),
        in_specs=[anywhere()] * 7 + [vmem()] * 3,
        out_specs=(vmem(),) * 6,
        scratch_shapes=[
            pltpu.VMEM((VEC, LEAVES * LEAF), F32),
            pltpu.VMEM((3, LEAVES * LEAF), F32),
            pltpu.VMEM((LEAVES, RANK, LEAF), F32),
            pltpu.VMEM((30, RANK, RANK), F32),
            pltpu.VMEM((3, PAIRS * 128), F32),
            pltpu.VMEM((3, UPN * RANK), F32),
            pltpu.VMEM((8, 128), jnp.int32),
            pltpu.VMEM((8, 128), jnp.int32),
            pltpu.VMEM((18 * LEAF, DEPTH), BF16),
            pltpu.VMEM((DEPTH, 18 * LEAF), BF16),
            pltpu.VMEM((2 * VEC, 18 * LEAF), BF16),
            pltpu.VMEM((2, VEC + 8, LEAF), F32),
            pltpu.VMEM((2, VEC + 8, LEAF), F32),
            pltpu.VMEM((PAY_ROWS, 128), F32),
            pltpu.VMEM((PAIRS * 8, 128), F32),
            pltpu.VMEM((RANK * RANK, UPN), F32),
            pltpu.VMEM((48 * RANK, RANK), F32),
            pltpu.VMEM((44, VEC, RANK), F32),
            pltpu.VMEM((UPPER, VEC, RANK), F32),
            pltpu.SemaphoreType.DMA((n_remote,)),
            pltpu.SemaphoreType.DMA((n_remote,)),
            pltpu.SemaphoreType.DMA((16,)),
        ],
        compiler_params=pltpu.CompilerParams(
            collective_id=0, has_side_effects=True, vmem_limit_bytes=63 << 20
        ),
    )(vectors, points, leaf_bases, lt, skel_points, up_rows, up_points, sources, targets, live_counts)

    partial = pl.pallas_call(
        couple_kernel,
        out_shape=shape(PTS, COEF_ROWS, 128),
        in_specs=[anywhere()] * 4,
        out_specs=vmem(),
        scratch_shapes=[
            pltpu.VMEM((LEAFS, PAY_ROWS, 128), F32),
            pltpu.VMEM((PTS, PAIRS * 8, 128), F32),
            pltpu.SMEM((LEAFS, 8, 128), jnp.int32),
            pltpu.SMEM((PTS, 8, 128), jnp.int32),
            pltpu.SemaphoreType.DMA((LEAFS + 3,)),
            pltpu.VMEM((LEAFS * GROUPS * 4 * RANK, 128), BF16),
            pltpu.VMEM((LEAFS * NODES * DEPTH, 128), BF16),
            pltpu.VMEM(((NODES + 1) * RANK, 2 * DEPTH), BF16),
            pltpu.VMEM((8, 16, 128), BF16),
            pltpu.VMEM((512, 128), BF16),
            pltpu.VMEM((LEAFS * RANK, 128), F32),
            pltpu.VMEM((LEAFS * RANK, 3 * 128), BF16),
            pltpu.VMEM(((NODES + 1) * RANK, 128), F32),
            pltpu.VMEM(((NODES + 1) * RANK, 128), F32),
        ],
        compiler_params=pltpu.CompilerParams(vmem_limit_bytes=63 << 20),
    )(gathered, tp, scg, tcg)

    return pl.pallas_call(
        scatter_kernel,
        out_shape=shape(VEC, LEAVES * LEAF),
        in_specs=[anywhere()] * 5,
        out_specs=vmem(),
        scratch_shapes=[
            pltpu.VMEM((4, COEF_ROWS, 128), F32),
            pltpu.VMEM((VEC, RANK), F32),
            pltpu.VMEM((30, RANK, RANK), F32),
            pltpu.VMEM((LEAVES, RANK, LEAF), F32),
            pltpu.VMEM((VEC, LEAVES * LEAF), F32),
            pltpu.VMEM((4, COEF_ROWS, 128), F32),
            pltpu.VMEM((COEF_ROWS, 128), F32),
            pltpu.VMEM((2, COEF_ROWS, 128), F32),
            pltpu.VMEM((4, COEF_ROWS, 128), F32),
            pltpu.SemaphoreType.DMA((8,)),
            pltpu.SemaphoreType.DMA((8,)),
            pltpu.SemaphoreType.DMA((8,)),
        ],
        compiler_params=pltpu.CompilerParams(
            collective_id=1, has_side_effects=True, vmem_limit_bytes=63 << 20
        ),
    )(partial, far, lt, leaf_bases, near)


def solution(mesh):
    both = ("leaf", "pts")
    return jax.shard_map(
        on_device,
        mesh=mesh,
        in_specs=(
            P(None, both),
            P(None, both),
            P(both, None, None),
            P(both, None, None, None),
            P(None, both),
            P(),
            P(),
            P(None, both, None, None),
            P(None, both, None, None),
            P(None, both, None),
        ),
        out_specs=P(None, both),
        check_vma=False,
    )
```

```python
import functools
import math

import jax
import jax.numpy as jnp
from jax import lax
from jax.experimental import pallas as pl
from jax.experimental.pallas import tpu as pltpu
from jax.sharding import PartitionSpec as P

F32 = jnp.float32
BF16 = jnp.bfloat16
MESH = pl.DeviceIdType.MESH
LN2 = math.log(2.0)
KAPPA = math.sqrt(3.0) / 0.3 / LN2
TINY = 1e-30

VEC = 32
RANK = 64
LEAF = 256
LEAVES = 16
PTS = 8
LEAFS = 16
PAIRS = 14
NODES = 28
COEF_ROWS = PAIRS * VEC
PAY_ROWS = COEF_ROWS + 48
UPPER = 7
UPN = 254
TREE = (0, 8, 12, 14, 30, 38, 42, 44)
GROUPS = NODES // 4
DEPTH = 48
NN = (((1,), (0,)), ((), ()))
NT = (((1,), (1,)), ((), ()))


def dg(a, b, dims):
    return lax.dot_general(a, b, dims, preferred_element_type=F32)


def split(x):
    hi = x.astype(BF16)
    return hi, (x - hi.astype(F32)).astype(BF16)


def dot3(a, b, dims):
    ah, al = split(a)
    bh, bl = split(b)
    return dg(ah, bh, dims) + (dg(ah, bl, dims) + dg(al, bh, dims))


def split3(x):
    h = x.astype(BF16).astype(F32)
    r = x - h
    m = r.astype(BF16).astype(F32)
    return h, m, r - m


def scaled(pts):
    return (pts - 0.5) * KAPPA


def forms(x):
    n = x.shape[1]
    x = jnp.concatenate([x, jnp.zeros((5, n), F32)], axis=0)
    q = jnp.sum(x * x, axis=0, keepdims=True)
    row = lax.broadcasted_iota(jnp.int32, (8, n), 0)
    w = jnp.where(row < 3, x, jnp.where(row == 3, 1.0, jnp.where(row == 4, q, 0.0)))
    u = jnp.where(row < 3, -2.0 * x, jnp.where(row == 3, q, jnp.where(row == 4, 1.0, 0.0)))
    return u, w


def stack_u(u):
    h, m, l = split3(u)
    return jnp.concatenate([h, h, m, m, h, l], axis=0)


def stack_w(w):
    h, m, l = split3(w)
    return jnp.concatenate([h, m, h, m, l, h], axis=0)


def matern(squared):
    squared = jnp.maximum(squared, TINY)
    t = squared * lax.rsqrt(squared)
    return (1.0 + LN2 * t) * jnp.exp2(-t)


def pair_matrix(lt_ref, n):
    return jnp.concatenate([lt_ref[2 * n], lt_ref[2 * n + 1]], axis=1)


def up_offset(u):
    return 0 if u == 0 else 256 - (128 >> (u - 1))


def gather_kernel(
    vec_hbm, pts_hbm, base_hbm, lt_hbm, skel_hbm, upt_ref, upp_hbm, src_ref, tgt_ref, live_ref,
    g_ref, near_ref, far_ref, tp_ref, scg_ref, tcg_ref,
    vec_ref, pts_ref, base_ref, lt_ref, skel_ref, upp_ref, sc_ref, tc_ref, u_scr, w_scr, v_scr, halo_src, halo_dst, pay, tpay, up_all, ut, tree, sf,
    ssem, rsem, lsem,
):
    leaf = lax.axis_index("leaf")
    p = lax.axis_index("pts")
    me = leaf * PTS + p
    y = leaf // 4
    z = lax.rem(leaf, 4)
    nxt = lax.rem(me + 1, 128)
    prv = lax.rem(me + 127, 128)
    nxt_dev = (nxt // PTS, lax.rem(nxt, PTS))
    prv_dev = (prv // PTS, lax.rem(prv, PTS))

    barrier = pltpu.get_barrier_semaphore()
    for k in range(1, LEAFS):
        pl.semaphore_signal(barrier, inc=1, device_id=(leaf ^ k, p), device_id_type=MESH)
    for k in range(1, PTS):
        pl.semaphore_signal(barrier, inc=1, device_id=(leaf, p ^ k), device_id_type=MESH)
    pl.semaphore_signal(barrier, inc=1, device_id=nxt_dev, device_id_type=MESH)
    pl.semaphore_signal(barrier, inc=1, device_id=prv_dev, device_id_type=MESH)

    counter = [0]
    sends = []

    def remote(src, dst, dev):
        i = counter[0]
        counter[0] += 1
        copy = pltpu.make_async_remote_copy(
            src_ref=src, dst_ref=dst, send_sem=ssem.at[i], recv_sem=rsem.at[i],
            device_id=dev, device_id_type=MESH,
        )
        copy.start()
        sends.append(copy)
        return copy

    locals_ = []

    def local(src, dst):
        copy = pltpu.make_async_copy(src, dst, lsem.at[len(locals_)])
        copy.start()
        locals_.append(copy)

    for src, dst in (
        (skel_hbm, skel_ref), (vec_hbm, vec_ref), (base_hbm, base_ref), (lt_hbm, lt_ref),
        (pts_hbm, pts_ref), (upp_hbm, upp_ref), (upt_ref, up_all),
    ):
        local(src, dst)

    sc_ref[...] = jnp.zeros_like(sc_ref)
    tc_ref[...] = jnp.zeros_like(tc_ref)
    for lev in range(3):
        shift = LEAVES * 2 - (LEAVES * 2 >> lev) - me * (LEAVES >> lev)
        for k in range(2):
            row = slice(2 * lev + k, 2 * lev + k + 1)
            sc_ref[row] = src_ref[lev, k:k + 1] + shift
            tc_ref[row] = jnp.where(k < live_ref[lev], tgt_ref[lev, k:k + 1] + shift, NODES)

    locals_[0].wait()
    pay[PAY_ROWS - 8:PAY_ROWS] = jnp.zeros((8, 128), F32)
    for a in range(PAIRS):
        x = scaled(skel_ref[:, a * 128:(a + 1) * 128])
        tpay[a * 8:(a + 1) * 8] = forms(x)[0]
        for c in range(3):
            row = COEF_ROWS + c * PAIRS + a
            pay[row:row + 1] = x[c:c + 1]

    lows = (0, LEAVES // 4 * RANK)
    sizes = (LEAVES // 4 * RANK, PAY_ROWS - LEAVES // 4 * RANK)

    def lid(yy, zz):
        return lax.rem(yy + 4, 4) * 4 + lax.rem(zz + 4, 4)

    def near_id(h, stage, step):
        return lid(y, z + step) if (h == 0) == (stage == 0) else lid(y + step, z)

    def block_id(h, first, second):
        return lid(y + second, z + first) if h == 0 else lid(y + first, z + second)

    stage1 = {}
    stage2 = {}

    def begin(h):
        rows = pl.ds(lows[h], sizes[h])
        for step in (1, -1):
            stage1[h, step] = remote(
                pay.at[rows], g_ref.at[leaf, rows], (near_id(h, 0, step), p)
            )

    def spread(h, first):
        rows = pl.ds(lows[h], sizes[h])
        blk = near_id(h, 0, first)
        src = pay.at[rows] if first == 0 else g_ref.at[blk, rows]
        for step in (1, -1):
            stage2[h, first, step] = remote(
                src, g_ref.at[blk, rows], (near_id(h, 1, step), p)
            )

    def forward(h, stage, blk_minus, blk_plus, got_minus, got_plus):
        part = sizes[h] // 16 * 8
        got_minus.wait_recv()
        rows = pl.ds(lows[h], part)
        one = remote(g_ref.at[blk_minus, rows], g_ref.at[blk_minus, rows], (near_id(h, stage, 1), p))
        got_plus.wait_recv()
        rows = pl.ds(lows[h] + part, sizes[h] - part)
        two = remote(g_ref.at[blk_plus, rows], g_ref.at[blk_plus, rows], (near_id(h, stage, -1), p))
        return one, two

    for i in (1, 2, 3):
        locals_[i].wait()
    level = [
        dot3(base_ref[n], vec_ref[:, n * LEAF:(n + 1) * LEAF], NT) for n in range(LEAVES)
    ]
    base = 0
    row = 0
    while len(level) > 1:
        if row < COEF_ROWS:
            for g in range(len(level) // 4):
                pay[row:row + RANK] = jnp.concatenate(level[4 * g:4 * g + 4], axis=1)
                row += RANK
        if row == sizes[0]:
            pl.semaphore_wait(barrier, LEAFS + PTS)
            begin(0)
            spread(0, 0)
        if row == COEF_ROWS and len(level) == 4:
            begin(1)
            spread(1, 0)
        level = [
            dot3(
                pair_matrix(lt_ref, base + i),
                jnp.concatenate([level[2 * i], level[2 * i + 1]], axis=0),
                NN,
            )
            for i in range(len(level) // 2)
        ]
        base += len(level)
    root = level[0].T
    tree[p] = root
    roots = [remote(tree.at[p], tree.at[p], (leaf, p ^ k)) for k in range(1, PTS)]

    local(pay, g_ref.at[leaf])

    r48 = lax.broadcasted_iota(jnp.int32, (48, UPN), 0)
    c48 = lax.broadcasted_iota(jnp.int32, (48, UPN), 1)
    want = jnp.where(
        r48 < 8, leaf * 8 + r48,
        jnp.where(r48 < 12, 120 + leaf * 4 + r48, jnp.where(r48 < 14, 180 + leaf * 2 + r48, 210 + r48)),
    )
    pick = (c48 == want).astype(F32).astype(BF16)

    def pick_rows(lo, hi):
        @pl.loop(lo, hi)
        def _(r):
            halves = [
                split(up_all[pl.ds(pl.multiple_of(r * 512 + i * 128, 128), 128), :])
                for i in range(4)
            ]
            got = [dg(pick, h, NT) + dg(pick, l, NT) for h, l in halves]
            for i, x in enumerate(got):
                ut[pl.ds(8 * r + 2 * i, 48, stride=RANK), :] = x[:, :RANK]
                ut[pl.ds(8 * r + 2 * i + 1, 48, stride=RANK), :] = x[:, RANK:]

    opposite = {}

    def step_a():
        for h in range(2):
            opposite[h] = forward(
                h, 0, near_id(h, 0, -1), near_id(h, 0, 1), stage1[h, 1], stage1[h, -1]
            )
            spread(h, -1)
            spread(h, 1)

    def step_b():
        for h in range(2):
            opposite[h][0].wait_recv()
            opposite[h][1].wait_recv()
            spread(h, 2)

    last = []

    def step_c(first):
        for h in range(2):
            last.extend(
                forward(
                    h, 1, block_id(h, first, -1), block_id(h, first, 1),
                    stage2[h, first, 1], stage2[h, first, -1],
                )
            )

    def matrix(n):
        return ut[pl.ds(pl.multiple_of(n * RANK, RANK), RANK), :]

    def parent(n):
        return dot3(
            jnp.concatenate([tree[n], tree[n + 1]], axis=1),
            jnp.concatenate([matrix(n), matrix(n + 1)], axis=1),
            NT,
        )

    def raise_level(u):
        return [parent(TREE[u] + 2 * i) for i in range((TREE[u + 1] - TREE[u]) // 2)]

    def own_node(u):
        return p >> u if u < 3 else leaf >> (u - 3)

    def lower_levels():
        for c in roots:
            c.wait_recv()
        for u in range(2):
            for i, x in enumerate(raise_level(u)):
                tree[TREE[u + 1] + i] = x
        mine = TREE[3] + leaf
        tree[mine] = raise_level(2)[0]
        return [remote(tree.at[mine], tree.at[mine], (leaf ^ k, p)) for k in range(1, LEAFS)]

    def upper_levels(tops):
        for c in tops:
            c.wait_recv()
        for u in range(3, 6):
            for i, x in enumerate(raise_level(u)):
                tree[TREE[u + 1] + i] = x

    def sibling_fields():
        lane_left = lax.broadcasted_iota(jnp.int32, (VEC, 2 * RANK), 1) < RANK
        distances = []
        for u in range(UPPER):
            first = lax.shift_right_logical(me, u + 1) * 2
            col = pl.multiple_of((up_offset(u) + first) * RANK, 128)
            u8, w8 = forms(scaled(upp_ref[:, pl.ds(col, 128)]))
            distances.append(dg(stack_u(u8).T.astype(BF16), stack_w(w8).astype(BF16), NN))
        kernels = [matern(x) for x in distances]
        for u in range(UPPER):
            left_side = lax.rem(own_node(u), 2) == 0
            sib = tree[TREE[u] + (own_node(u) ^ 1)]
            pair = jnp.concatenate([sib, sib], axis=1)
            only_sib = jnp.where(jnp.logical_xor(lane_left, left_side), pair, 0.0)
            out = dot3(only_sib, kernels[u], NN)
            sf[u] = jnp.where(left_side, out[:, :RANK], out[:, RANK:])

    def prepare(slot, vec, pts):
        vh, vl = split(vec)
        lanes = pl.ds(pl.multiple_of(slot * LEAF, LEAF), LEAF)
        v_scr[0:VEC, lanes] = vh
        v_scr[VEC:2 * VEC, lanes] = vl
        u8, w8 = forms(scaled(pts))
        w_scr[:, lanes] = stack_w(w8).astype(BF16)
        u_scr[lanes, :] = stack_u(u8).T.astype(BF16)

    def near(m):
        lanes = pl.ds(pl.multiple_of(m * LEAF, LEAF), LEAF)
        w = w_scr[:, lanes]
        total = None
        for b in range(3):
            src = pl.ds(pl.multiple_of((m - 1 + b) * LEAF, LEAF), LEAF)
            kh, kl = split(matern(dg(u_scr[src, :], w, NN)))
            v = v_scr[:, src]
            big = dg(v, kh, NN)
            part = big[:VEC] + (big[VEC:] + dg(v[:VEC], kl, NN))
            total = part if total is None else total + part
        near_ref[:, pl.ds(pl.multiple_of((m - 1) * LEAF, LEAF), LEAF)] = total

    def near_span(lo, hi):
        @pl.loop(lo, hi)
        def _(m):
            near(m)

    step_a()
    locals_[6].wait()
    pick_rows(0, 4)
    step_b()
    pick_rows(4, 8)
    tops = lower_levels()
    step_c(0)
    for i in (4, 5):
        locals_[i].wait()
    for side, off in ((0, 0), (1, (LEAVES - 1) * LEAF)):
        halo_src[side, 0:VEC] = vec_ref[:, off:off + LEAF]
        halo_src[side, VEC:VEC + 8] = jnp.concatenate(
            [pts_ref[:, off:off + LEAF], jnp.zeros((5, LEAF), F32)], axis=0
        )
    h0 = remote(halo_src.at[0], halo_dst.at[1], prv_dev)
    h1 = remote(halo_src.at[1], halo_dst.at[0], nxt_dev)
    arrivals = []
    for k in range(1, PTS):
        arrivals.append(remote(tpay, tp_ref.at[p], (leaf, p ^ k)))
        arrivals.append(remote(tc_ref, tcg_ref.at[p], (leaf, p ^ k)))
    for k in range(1, LEAFS):
        arrivals.append(remote(sc_ref, scg_ref.at[leaf], (leaf ^ k, p)))
    local(tpay, tp_ref.at[p])
    local(tc_ref, tcg_ref.at[p])
    local(sc_ref, scg_ref.at[leaf])


    @pl.loop(0, LEAVES)
    def _(m):
        lanes = pl.ds(pl.multiple_of(m * LEAF, LEAF), LEAF)
        prepare(m + 1, vec_ref[:, lanes], pts_ref[:, lanes])

    near_span(2, 6)
    step_c(-1)
    near_span(6, 10)
    step_c(1)
    near_span(10, 12)
    step_c(2)
    upper_levels(tops)
    near_span(12, 16)
    sibling_fields()
    h0.wait_recv()
    h1.wait_recv()
    for side, slot, edge in ((0, 0, 0), (1, LEAVES + 1, 127)):
        vec = jnp.where(me == edge, 0.0, halo_dst[side, 0:VEC])
        prepare(slot, vec, halo_dst[side, VEC:VEC + 3])
    near(1)
    near(LEAVES)

    far = sf[UPPER - 1]
    for u in range(UPPER - 2, -1, -1):
        far = sf[u] + dot3(far, matrix(TREE[u] + own_node(u)), NN)
    far_ref[...] = far

    for c in arrivals:
        c.wait_recv()
    for c in last:
        c.wait_recv()
    for c in sends:
        c.wait_send()
    for c in locals_[7:]:
        c.wait()


def couple_kernel(
    g_hbm, tp_hbm, sc_hbm, tc_hbm, o_ref, g_ref, tp_ref, sc_ref, tc_ref, sem, ct, wt, ut, masks, sums, d_scr, k_scr, acc_a, acc_b, used,
):
    leaf = lax.axis_index("leaf")
    p = lax.axis_index("pts")
    lane = lax.broadcasted_iota(jnp.int32, (16, 128), 1)
    low = lax.broadcasted_iota(jnp.int32, (RANK, 128), 1) < RANK

    def rows_of(index, size):
        return pl.ds(pl.multiple_of(index * size, size), size)

    blocks = [pltpu.make_async_copy(g_hbm.at[s], g_ref.at[s], sem.at[s]) for s in range(LEAFS)]
    others = [
        pltpu.make_async_copy(a, b, sem.at[LEAFS + i])
        for i, (a, b) in enumerate(((tp_hbm, tp_ref), (sc_hbm, sc_ref), (tc_hbm, tc_ref)))
    ]
    for copy in blocks + others:
        copy.start()

    for q in range(4):
        masks[q] = (lane // VEC == q).astype(F32).astype(BF16)
    for q in range(2):
        masks[4 + q] = (lane // RANK == q).astype(F32).astype(BF16)
    r = lax.broadcasted_iota(jnp.int32, (512, 128), 0)
    c = lax.broadcasted_iota(jnp.int32, (512, 128), 1)
    sums[...] = jnp.logical_and(
        lax.rem(r, VEC) == lax.rem(c, VEC), r // 128 == c // VEC
    ).astype(F32).astype(BF16)

    def masked(x, m):
        return (x.reshape(-1, 16, 128) * masks[m][None]).reshape(x.shape)

    for copy in others:
        copy.wait()

    def fill(s, count):
        pltpu.make_async_copy(g_hbm.at[s], g_ref.at[s], sem.at[s]).wait()
        for d in range(PTS):
            for row in range(6):
                r = tc_ref[d, row, s * PTS + p]
                n = s * NODES + sc_ref[s, row, leaf * PTS + d]
                used[count] = n * 256 + (r + d * (NODES + 1))
                count = count + (r < NODES).astype(jnp.int32)
        for g in range(GROUPS):
            c = g_ref[s, g * RANK:(g + 1) * RANK, :]
            for j in range(2):
                h, l = split(pltpu.roll(c, RANK, 1) if j else c)
                rows = (s * GROUPS + g) * 2 + j
                ct[rows_of(rows, 2 * RANK), :] = jnp.concatenate([h, l], axis=0)
        for a in range(PAIRS):
            x = jnp.concatenate(
                [
                    g_ref[s, COEF_ROWS + c * PAIRS + a:COEF_ROWS + c * PAIRS + a + 1, :]
                    for c in range(3)
                ],
                axis=0,
            )
            w = forms(x)[1]
            for j in range(2):
                rows = (s * PAIRS + a) * 2 + j
                wt[rows_of(rows, DEPTH), :] = stack_w(
                    pltpu.roll(w, RANK, 1) if j else w
                ).astype(BF16)

        return count

    total = lax.fori_loop(0, LEAFS, fill, jnp.int32(0))
    for i in range(2 * LEAFS):
        used[total + i] = NODES
    slot_a = lax.broadcasted_iota(jnp.int32, (RANK, 2 * DEPTH), 1) < DEPTH

    @pl.loop(0, PTS)
    def _(d):
        first = d * (NODES + 1)
        for a in range(PAIRS):
            t = stack_u(tp_ref[d, a * 8:(a + 1) * 8, :])
            rows = pl.ds(pl.multiple_of((first + 2 * a) * RANK, RANK), 2 * RANK)
            ut[rows, :] = jnp.concatenate([t, t], axis=0).T.astype(BF16)
        ut[rows_of(first + NODES, RANK), :] = jnp.zeros((RANK, 2 * DEPTH), BF16)
        rows = pl.ds(pl.multiple_of(first * RANK, RANK), (NODES + 1) * RANK)
        acc_a[rows, :] = jnp.zeros(((NODES + 1) * RANK, 128), F32)
        acc_b[rows, :] = jnp.zeros(((NODES + 1) * RANK, 128), F32)

    def step(g, carry):
        ids = []
        for t in range(LEAFS):
            a = used[g * 2 * LEAFS + 2 * t]
            b = used[g * 2 * LEAFS + 2 * t + 1]
            ids.append((a >> 8, b >> 8, rows_of(a & 255, RANK), rows_of(b & 255, RANK)))
        for s, (na, nb, ra, rb) in enumerate(ids):
            u = jnp.where(slot_a, ut[ra, :], ut[rb, :])
            wa = masked(wt[rows_of(na, DEPTH), :], 4)
            wb = masked(wt[rows_of(nb ^ 1, DEPTH), :], 5)
            d_scr[s * RANK:(s + 1) * RANK] = dg(u, jnp.concatenate([wa, wb], axis=0), NN)
        for s in range(LEAFS):
            h, l = split(matern(d_scr[s * RANK:(s + 1) * RANK]))
            k_scr[s * RANK:(s + 1) * RANK] = jnp.concatenate([h, l, h], axis=1)
        for s, (na, nb, ra, rb) in enumerate(ids):
            xa = masked(ct[rows_of(na >> 1, 2 * RANK), :], na & 1)
            xb = masked(ct[rows_of((nb >> 1) ^ 1, 2 * RANK), :], 2 + (nb & 1))
            high = jnp.concatenate([xa[:RANK], xb[:RANK]], axis=0)
            rest = jnp.concatenate([xa[RANK:], xb[RANK:]], axis=0)
            k = k_scr[s * RANK:(s + 1) * RANK]
            part = dg(k, jnp.concatenate([high, high, rest], axis=0), NN)
            acc_a[ra, :] += part
            acc_b[rb, :] += part
        return carry

    lax.fori_loop(0, (total + 2 * LEAFS - 1) >> 5, step, 0)

    @pl.loop(0, PTS)
    def _(d):
        for g in range(GROUPS):
            parts = []
            for q in range(4):
                rows = rows_of(d * (NODES + 1) + 4 * g + q, RANK)
                parts.append(jnp.where(low, acc_a[rows, :], acc_b[rows, :]))
            h, l = split(jnp.concatenate(parts, axis=1))
            o_ref[d, g * RANK:(g + 1) * RANK, :] = dg(h, sums[...], NN) + dg(l, sums[...], NN)


def scatter_kernel(
    acc_hbm, far_hbm, lt_hbm, base_hbm, near_hbm, out_ref,
    acc_ref, far_ref, lt_ref, base_ref, near_ref, from_core, s1, s2, work, ssem, rsem, lsem,
):
    leaf = lax.axis_index("leaf")
    p = lax.axis_index("pts")
    x = p // 2
    core = lax.rem(p, 2)
    sister = (leaf, p ^ 1)

    own_blocks = {}
    steps = (2, 1, 3, 0)
    for st in steps:
        blk = lax.rem(x + st, 4) * 2 + core
        own_blocks[st] = pltpu.make_async_copy(acc_hbm.at[blk], acc_ref.at[st], lsem.at[st])
        own_blocks[st].start()
    others = [
        pltpu.make_async_copy(a, b, lsem.at[4 + i])
        for i, (a, b) in enumerate(
            ((far_hbm, far_ref), (lt_hbm, lt_ref), (base_hbm, base_ref), (near_hbm, near_ref))
        )
    ]
    for copy in others:
        copy.start()

    def dev(step):
        return (leaf, lax.rem(x + step + 4, 4) * 2 + core)

    barrier = pltpu.get_barrier_semaphore()
    for d in (sister, dev(1), dev(-1)):
        pl.semaphore_signal(barrier, inc=1, device_id=d, device_id_type=MESH)
    pl.semaphore_wait(barrier, 3)

    sends = []

    def remote(src, dst, device):
        i = len(sends)
        copy = pltpu.make_async_remote_copy(
            src_ref=src, dst_ref=dst, send_sem=ssem.at[i], recv_sem=rsem.at[i],
            device_id=device, device_id_type=MESH,
        )
        copy.start()
        sends.append(copy)
        return copy

    half = COEF_ROWS // 2
    first = {}
    for st in steps:
        xx = lax.rem(x + st, 4)
        first[st] = remote(acc_hbm.at[xx * 2 + 1 - core], from_core.at[st], sister)

    def summed(st):
        first[st].wait_recv()
        own_blocks[st].wait()
        return acc_ref[st] + from_core[st]

    work[0] = summed(2)
    a1 = remote(work.at[0, pl.ds(0, half)], s1.at[pl.ds(0, half)], dev(1))
    b1 = remote(work.at[0, pl.ds(half, half)], s1.at[pl.ds(half, half)], dev(-1))
    work[1] = summed(1)
    work[2] = summed(3)
    a1.wait_recv()
    work[1, 0:half] += s1[0:half]
    a2 = remote(work.at[1], s2.at[0], dev(1))
    b1.wait_recv()
    work[2, half:] += s1[half:]
    b2 = remote(work.at[2], s2.at[1], dev(-1))

    def down(node, n):
        return dot3(node, pair_matrix(lt_ref, n), NN)

    for copy in others:
        copy.wait()
    top = down(far_ref[...], 14)
    level2 = [down(top[:, :RANK], 12), down(top[:, RANK:], 13)]
    own = summed(0)
    a2.wait_recv()
    b2.wait_recv()
    work[3] = own + (s2[0] + s2[1])

    turned = [work[3, g * RANK:(g + 1) * RANK].T for g in range(GROUPS)]

    def coupling(a):
        t = turned[a // 2]
        r = (a % 2) * 2 * VEC
        return jnp.concatenate([t[r:r + VEC], t[r + VEC:r + 2 * VEC]], axis=1)

    pairs = [level2[i] + coupling(12 + i) for i in range(2)]
    pairs = [
        down(pairs[i // 2][:, (i % 2) * RANK:(i % 2 + 1) * RANK], 8 + i) + coupling(8 + i)
        for i in range(4)
    ]
    pairs = [
        down(pairs[i // 2][:, (i % 2) * RANK:(i % 2 + 1) * RANK], i) + coupling(i)
        for i in range(8)
    ]
    for m in range(LEAVES):
        c = pairs[m // 2][:, (m % 2) * RANK:(m % 2 + 1) * RANK]
        cols = slice(m * LEAF, (m + 1) * LEAF)
        out_ref[:, cols] = near_ref[:, cols] + dot3(c, base_ref[m], NN)
    for c in sends:
        c.wait_send()


def vmem():
    return pl.BlockSpec(memory_space=pltpu.VMEM)


def anywhere():
    return pl.BlockSpec(memory_space=pl.ANY)


def shape(*dims, dtype=F32):
    return jax.ShapeDtypeStruct(dims, dtype)


def on_device(
    vectors, points, leaf_bases, local_transfer, skel_points, up_transfer, up_points,
    source_ids, target_ids, live_counts,
):
    sources = jnp.swapaxes(source_ids[:, 0], 1, 2)
    targets = jnp.swapaxes(target_ids[:, 0], 1, 2)
    lt = local_transfer[0]
    up_rows = jnp.transpose(up_transfer, (1, 2, 0)).reshape(RANK * RANK, UPN)
    n_remote = 112

    gathered, near, far, tp, scg, tcg = pl.pallas_call(
        gather_kernel,
        out_shape=(
            shape(LEAFS, PAY_ROWS, 128), shape(VEC, LEAVES * LEAF), shape(VEC, RANK),
            shape(PTS, PAIRS * 8, 128), shape(LEAFS, 8, 128, dtype=jnp.int32),
            shape(PTS, 8, 128, dtype=jnp.int32),
        ),
        in_specs=[anywhere()] * 7 + [vmem()] * 3,
        out_specs=(vmem(),) * 6,
        scratch_shapes=[
            pltpu.VMEM((VEC, LEAVES * LEAF), F32),
            pltpu.VMEM((3, LEAVES * LEAF), F32),
            pltpu.VMEM((LEAVES, RANK, LEAF), F32),
            pltpu.VMEM((30, RANK, RANK), F32),
            pltpu.VMEM((3, PAIRS * 128), F32),
            pltpu.VMEM((3, UPN * RANK), F32),
            pltpu.VMEM((8, 128), jnp.int32),
            pltpu.VMEM((8, 128), jnp.int32),
            pltpu.VMEM((18 * LEAF, DEPTH), BF16),
            pltpu.VMEM((DEPTH, 18 * LEAF), BF16),
            pltpu.VMEM((2 * VEC, 18 * LEAF), BF16),
            pltpu.VMEM((2, VEC + 8, LEAF), F32),
            pltpu.VMEM((2, VEC + 8, LEAF), F32),
            pltpu.VMEM((PAY_ROWS, 128), F32),
            pltpu.VMEM((PAIRS * 8, 128), F32),
            pltpu.VMEM((RANK * RANK, UPN), F32),
            pltpu.VMEM((48 * RANK, RANK), F32),
            pltpu.VMEM((44, VEC, RANK), F32),
            pltpu.VMEM((UPPER, VEC, RANK), F32),
            pltpu.SemaphoreType.DMA((n_remote,)),
            pltpu.SemaphoreType.DMA((n_remote,)),
            pltpu.SemaphoreType.DMA((16,)),
        ],
        compiler_params=pltpu.CompilerParams(
            collective_id=0, has_side_effects=True, vmem_limit_bytes=63 << 20
        ),
    )(vectors, points, leaf_bases, lt, skel_points, up_rows, up_points, sources, targets, live_counts)

    partial = pl.pallas_call(
        couple_kernel,
        out_shape=shape(PTS, COEF_ROWS, 128),
        in_specs=[anywhere()] * 4,
        out_specs=vmem(),
        scratch_shapes=[
            pltpu.VMEM((LEAFS, PAY_ROWS, 128), F32),
            pltpu.VMEM((PTS, PAIRS * 8, 128), F32),
            pltpu.SMEM((LEAFS, 8, 128), jnp.int32),
            pltpu.SMEM((PTS, 8, 128), jnp.int32),
            pltpu.SemaphoreType.DMA((LEAFS + 3,)),
            pltpu.VMEM((LEAFS * GROUPS * 4 * RANK, 128), BF16),
            pltpu.VMEM((LEAFS * NODES * DEPTH, 128), BF16),
            pltpu.VMEM((PTS * (NODES + 1) * RANK, 2 * DEPTH), BF16),
            pltpu.VMEM((8, 16, 128), BF16),
            pltpu.VMEM((512, 128), BF16),
            pltpu.VMEM((LEAFS * RANK, 128), F32),
            pltpu.VMEM((LEAFS * RANK, 3 * 128), BF16),
            pltpu.VMEM((PTS * (NODES + 1) * RANK, 128), F32),
            pltpu.VMEM((PTS * (NODES + 1) * RANK, 128), F32),
            pltpu.SMEM((1024,), jnp.int32),
        ],
        compiler_params=pltpu.CompilerParams(vmem_limit_bytes=63 << 20),
    )(gathered, tp, scg, tcg)

    return pl.pallas_call(
        scatter_kernel,
        out_shape=shape(VEC, LEAVES * LEAF),
        in_specs=[anywhere()] * 5,
        out_specs=vmem(),
        scratch_shapes=[
            pltpu.VMEM((4, COEF_ROWS, 128), F32),
            pltpu.VMEM((VEC, RANK), F32),
            pltpu.VMEM((30, RANK, RANK), F32),
            pltpu.VMEM((LEAVES, RANK, LEAF), F32),
            pltpu.VMEM((VEC, LEAVES * LEAF), F32),
            pltpu.VMEM((4, COEF_ROWS, 128), F32),
            pltpu.VMEM((COEF_ROWS, 128), F32),
            pltpu.VMEM((2, COEF_ROWS, 128), F32),
            pltpu.VMEM((4, COEF_ROWS, 128), F32),
            pltpu.SemaphoreType.DMA((8,)),
            pltpu.SemaphoreType.DMA((8,)),
            pltpu.SemaphoreType.DMA((8,)),
        ],
        compiler_params=pltpu.CompilerParams(
            collective_id=1, has_side_effects=True, vmem_limit_bytes=63 << 20
        ),
    )(partial, far, lt, leaf_bases, near)


def solution(mesh):
    both = ("leaf", "pts")
    return jax.shard_map(
        on_device,
        mesh=mesh,
        in_specs=(
            P(None, both),
            P(None, both),
            P(both, None, None),
            P(both, None, None, None),
            P(None, both),
            P(),
            P(),
            P(None, both, None, None),
            P(None, both, None, None),
            P(None, both, None),
        ),
        out_specs=P(None, both),
        check_vma=False,
    )
```

```python
import functools
import math

import jax
import jax.numpy as jnp
from jax import lax
from jax.experimental import pallas as pl
from jax.experimental.pallas import tpu as pltpu
from jax.sharding import PartitionSpec as P

F32 = jnp.float32
BF16 = jnp.bfloat16
MESH = pl.DeviceIdType.MESH
LN2 = math.log(2.0)
KAPPA = math.sqrt(3.0) / 0.3 / LN2
TINY = 1e-30

VEC = 32
RANK = 64
LEAF = 256
LEAVES = 16
PTS = 8
LEAFS = 16
PAIRS = 14
NODES = 28
COEF_ROWS = PAIRS * VEC
PAY_ROWS = COEF_ROWS + 48
UPPER = 7
UPN = 254
TREE = (0, 8, 12, 14, 30, 38, 42, 44)
GROUPS = NODES // 4
BATCH = 32
DEPTH = 48
NN = (((1,), (0,)), ((), ()))
NT = (((1,), (1,)), ((), ()))


def dg(a, b, dims):
    return lax.dot_general(a, b, dims, preferred_element_type=F32)


def split(x):
    hi = x.astype(BF16)
    return hi, (x - hi.astype(F32)).astype(BF16)


def dot3(a, b, dims):
    ah, al = split(a)
    bh, bl = split(b)
    return dg(ah, bh, dims) + (dg(ah, bl, dims) + dg(al, bh, dims))


def split3(x):
    h = x.astype(BF16).astype(F32)
    r = x - h
    m = r.astype(BF16).astype(F32)
    return h, m, r - m


def scaled(pts):
    return (pts - 0.5) * KAPPA


def forms(x):
    n = x.shape[1]
    x = jnp.concatenate([x, jnp.zeros((5, n), F32)], axis=0)
    q = jnp.sum(x * x, axis=0, keepdims=True)
    row = lax.broadcasted_iota(jnp.int32, (8, n), 0)
    w = jnp.where(row < 3, x, jnp.where(row == 3, 1.0, jnp.where(row == 4, q, 0.0)))
    u = jnp.where(row < 3, -2.0 * x, jnp.where(row == 3, q, jnp.where(row == 4, 1.0, 0.0)))
    return u, w


def stack_u(u):
    h, m, l = split3(u)
    return jnp.concatenate([h, h, m, m, h, l], axis=0)


def stack_w(w):
    h, m, l = split3(w)
    return jnp.concatenate([h, m, h, m, l, h], axis=0)


def matern(squared):
    squared = jnp.maximum(squared, TINY)
    t = squared * lax.rsqrt(squared)
    return (1.0 + LN2 * t) * jnp.exp2(-t)


def pair_matrix(lt_ref, n):
    return jnp.concatenate([lt_ref[2 * n], lt_ref[2 * n + 1]], axis=1)


def up_offset(u):
    return 0 if u == 0 else 256 - (128 >> (u - 1))


def gather_kernel(
    vec_hbm, pts_hbm, base_hbm, lt_hbm, skel_hbm, upt_ref, upp_hbm, src_ref, tgt_ref, live_ref,
    g_ref, near_ref, far_ref, tp_ref, scg_ref, tcg_ref,
    vec_ref, pts_ref, base_ref, lt_ref, skel_ref, upp_ref, sc_ref, tc_ref, u_scr, w_scr, v_scr, halo_src, halo_dst, pay, tpay, up_all, ut, tree, sf,
    ssem, rsem, lsem,
):
    leaf = lax.axis_index("leaf")
    p = lax.axis_index("pts")
    me = leaf * PTS + p
    y = leaf // 4
    z = lax.rem(leaf, 4)
    nxt = lax.rem(me + 1, 128)
    prv = lax.rem(me + 127, 128)
    nxt_dev = (nxt // PTS, lax.rem(nxt, PTS))
    prv_dev = (prv // PTS, lax.rem(prv, PTS))

    barrier = pltpu.get_barrier_semaphore()
    for k in range(1, LEAFS):
        pl.semaphore_signal(barrier, inc=1, device_id=(leaf ^ k, p), device_id_type=MESH)
    for k in range(1, PTS):
        pl.semaphore_signal(barrier, inc=1, device_id=(leaf, p ^ k), device_id_type=MESH)
    pl.semaphore_signal(barrier, inc=1, device_id=nxt_dev, device_id_type=MESH)
    pl.semaphore_signal(barrier, inc=1, device_id=prv_dev, device_id_type=MESH)

    counter = [0]
    sends = []

    def remote(src, dst, dev):
        i = counter[0]
        counter[0] += 1
        copy = pltpu.make_async_remote_copy(
            src_ref=src, dst_ref=dst, send_sem=ssem.at[i], recv_sem=rsem.at[i],
            device_id=dev, device_id_type=MESH,
        )
        copy.start()
        sends.append(copy)
        return copy

    locals_ = []

    def local(src, dst):
        copy = pltpu.make_async_copy(src, dst, lsem.at[len(locals_)])
        copy.start()
        locals_.append(copy)

    for src, dst in (
        (skel_hbm, skel_ref), (vec_hbm, vec_ref), (base_hbm, base_ref), (lt_hbm, lt_ref),
        (pts_hbm, pts_ref), (upp_hbm, upp_ref), (upt_ref, up_all),
    ):
        local(src, dst)

    sc_ref[...] = jnp.zeros_like(sc_ref)
    tc_ref[...] = jnp.zeros_like(tc_ref)
    for lev in range(3):
        shift = LEAVES * 2 - (LEAVES * 2 >> lev) - me * (LEAVES >> lev)
        for k in range(2):
            row = slice(2 * lev + k, 2 * lev + k + 1)
            sc_ref[row] = (src_ref[lev, k:k + 1] + (shift + leaf * NODES)) * 256
            target = jnp.where(k < live_ref[lev], tgt_ref[lev, k:k + 1] + shift, NODES)
            tc_ref[row] = target + p * (NODES + 1)

    locals_[0].wait()
    pay[PAY_ROWS - 8:PAY_ROWS] = jnp.zeros((8, 128), F32)
    for a in range(PAIRS):
        x = scaled(skel_ref[:, a * 128:(a + 1) * 128])
        tpay[a * 8:(a + 1) * 8] = forms(x)[0]
        for c in range(3):
            row = COEF_ROWS + c * PAIRS + a
            pay[row:row + 1] = x[c:c + 1]

    lows = (0, LEAVES // 4 * RANK)
    sizes = (LEAVES // 4 * RANK, PAY_ROWS - LEAVES // 4 * RANK)

    def lid(yy, zz):
        return lax.rem(yy + 4, 4) * 4 + lax.rem(zz + 4, 4)

    def near_id(h, stage, step):
        return lid(y, z + step) if (h == 0) == (stage == 0) else lid(y + step, z)

    def block_id(h, first, second):
        return lid(y + second, z + first) if h == 0 else lid(y + first, z + second)

    stage1 = {}
    stage2 = {}

    def begin(h):
        rows = pl.ds(lows[h], sizes[h])
        for step in (1, -1):
            stage1[h, step] = remote(
                pay.at[rows], g_ref.at[leaf, rows], (near_id(h, 0, step), p)
            )

    def spread(h, first):
        rows = pl.ds(lows[h], sizes[h])
        blk = near_id(h, 0, first)
        src = pay.at[rows] if first == 0 else g_ref.at[blk, rows]
        for step in (1, -1):
            stage2[h, first, step] = remote(
                src, g_ref.at[blk, rows], (near_id(h, 1, step), p)
            )

    def forward(h, stage, blk_minus, blk_plus, got_minus, got_plus):
        part = sizes[h] // 16 * 8
        got_minus.wait_recv()
        rows = pl.ds(lows[h], part)
        one = remote(g_ref.at[blk_minus, rows], g_ref.at[blk_minus, rows], (near_id(h, stage, 1), p))
        got_plus.wait_recv()
        rows = pl.ds(lows[h] + part, sizes[h] - part)
        two = remote(g_ref.at[blk_plus, rows], g_ref.at[blk_plus, rows], (near_id(h, stage, -1), p))
        return one, two

    for i in (1, 2, 3):
        locals_[i].wait()
    level = [
        dot3(base_ref[n], vec_ref[:, n * LEAF:(n + 1) * LEAF], NT) for n in range(LEAVES)
    ]
    base = 0
    row = 0
    while len(level) > 1:
        if row < COEF_ROWS:
            for g in range(len(level) // 4):
                pay[row:row + RANK] = jnp.concatenate(level[4 * g:4 * g + 4], axis=1)
                row += RANK
        if row == sizes[0]:
            pl.semaphore_wait(barrier, LEAFS + PTS)
            begin(0)
            spread(0, 0)
        if row == COEF_ROWS and len(level) == 4:
            begin(1)
            spread(1, 0)
        level = [
            dot3(
                pair_matrix(lt_ref, base + i),
                jnp.concatenate([level[2 * i], level[2 * i + 1]], axis=0),
                NN,
            )
            for i in range(len(level) // 2)
        ]
        base += len(level)
    root = level[0].T
    tree[p] = root
    roots = [remote(tree.at[p], tree.at[p], (leaf, p ^ k)) for k in range(1, PTS)]

    local(pay, g_ref.at[leaf])

    r48 = lax.broadcasted_iota(jnp.int32, (48, UPN), 0)
    c48 = lax.broadcasted_iota(jnp.int32, (48, UPN), 1)
    want = jnp.where(
        r48 < 8, leaf * 8 + r48,
        jnp.where(r48 < 12, 120 + leaf * 4 + r48, jnp.where(r48 < 14, 180 + leaf * 2 + r48, 210 + r48)),
    )
    pick = (c48 == want).astype(F32).astype(BF16)

    def pick_rows(lo, hi):
        @pl.loop(lo, hi)
        def _(r):
            halves = [
                split(up_all[pl.ds(pl.multiple_of(r * 512 + i * 128, 128), 128), :])
                for i in range(4)
            ]
            got = [dg(pick, h, NT) + dg(pick, l, NT) for h, l in halves]
            for i, x in enumerate(got):
                ut[pl.ds(8 * r + 2 * i, 48, stride=RANK), :] = x[:, :RANK]
                ut[pl.ds(8 * r + 2 * i + 1, 48, stride=RANK), :] = x[:, RANK:]

    opposite = {}

    def step_a():
        for h in range(2):
            opposite[h] = forward(
                h, 0, near_id(h, 0, -1), near_id(h, 0, 1), stage1[h, 1], stage1[h, -1]
            )
            spread(h, -1)
            spread(h, 1)

    def step_b():
        for h in range(2):
            opposite[h][0].wait_recv()
            opposite[h][1].wait_recv()
            spread(h, 2)

    last = []

    def step_c(first):
        for h in range(2):
            last.extend(
                forward(
                    h, 1, block_id(h, first, -1), block_id(h, first, 1),
                    stage2[h, first, 1], stage2[h, first, -1],
                )
            )

    def matrix(n):
        return ut[pl.ds(pl.multiple_of(n * RANK, RANK), RANK), :]

    def parent(n):
        return dot3(
            jnp.concatenate([tree[n], tree[n + 1]], axis=1),
            jnp.concatenate([matrix(n), matrix(n + 1)], axis=1),
            NT,
        )

    def raise_level(u):
        return [parent(TREE[u] + 2 * i) for i in range((TREE[u + 1] - TREE[u]) // 2)]

    def own_node(u):
        return p >> u if u < 3 else leaf >> (u - 3)

    def lower_levels():
        for c in roots:
            c.wait_recv()
        for u in range(2):
            for i, x in enumerate(raise_level(u)):
                tree[TREE[u + 1] + i] = x
        mine = TREE[3] + leaf
        tree[mine] = raise_level(2)[0]
        return [remote(tree.at[mine], tree.at[mine], (leaf ^ k, p)) for k in range(1, LEAFS)]

    def upper_levels(tops):
        for c in tops:
            c.wait_recv()
        for u in range(3, 6):
            for i, x in enumerate(raise_level(u)):
                tree[TREE[u + 1] + i] = x

    def sibling_fields():
        lane_left = lax.broadcasted_iota(jnp.int32, (VEC, 2 * RANK), 1) < RANK
        distances = []
        for u in range(UPPER):
            first = lax.shift_right_logical(me, u + 1) * 2
            col = pl.multiple_of((up_offset(u) + first) * RANK, 128)
            u8, w8 = forms(scaled(upp_ref[:, pl.ds(col, 128)]))
            distances.append(dg(stack_u(u8).T.astype(BF16), stack_w(w8).astype(BF16), NN))
        kernels = [matern(x) for x in distances]
        for u in range(UPPER):
            left_side = lax.rem(own_node(u), 2) == 0
            sib = tree[TREE[u] + (own_node(u) ^ 1)]
            pair = jnp.concatenate([sib, sib], axis=1)
            only_sib = jnp.where(jnp.logical_xor(lane_left, left_side), pair, 0.0)
            out = dot3(only_sib, kernels[u], NN)
            sf[u] = jnp.where(left_side, out[:, :RANK], out[:, RANK:])

    def prepare(slot, vec, pts):
        vh, vl = split(vec)
        lanes = pl.ds(pl.multiple_of(slot * LEAF, LEAF), LEAF)
        v_scr[0:VEC, lanes] = vh
        v_scr[VEC:2 * VEC, lanes] = vl
        u8, w8 = forms(scaled(pts))
        w_scr[:, lanes] = stack_w(w8).astype(BF16)
        u_scr[lanes, :] = stack_u(u8).T.astype(BF16)

    def near(m):
        lanes = pl.ds(pl.multiple_of(m * LEAF, LEAF), LEAF)
        w = w_scr[:, lanes]
        total = None
        for b in range(3):
            src = pl.ds(pl.multiple_of((m - 1 + b) * LEAF, LEAF), LEAF)
            kh, kl = split(matern(dg(u_scr[src, :], w, NN)))
            v = v_scr[:, src]
            big = dg(v, kh, NN)
            part = big[:VEC] + (big[VEC:] + dg(v[:VEC], kl, NN))
            total = part if total is None else total + part
        near_ref[:, pl.ds(pl.multiple_of((m - 1) * LEAF, LEAF), LEAF)] = total

    def near_span(lo, hi):
        @pl.loop(lo, hi)
        def _(m):
            near(m)

    step_a()
    locals_[6].wait()
    pick_rows(0, 4)
    step_b()
    pick_rows(4, 8)
    tops = lower_levels()
    step_c(0)
    for i in (4, 5):
        locals_[i].wait()
    for side, off in ((0, 0), (1, (LEAVES - 1) * LEAF)):
        halo_src[side, 0:VEC] = vec_ref[:, off:off + LEAF]
        halo_src[side, VEC:VEC + 8] = jnp.concatenate(
            [pts_ref[:, off:off + LEAF], jnp.zeros((5, LEAF), F32)], axis=0
        )
    h0 = remote(halo_src.at[0], halo_dst.at[1], prv_dev)
    h1 = remote(halo_src.at[1], halo_dst.at[0], nxt_dev)
    arrivals = []
    for k in range(1, PTS):
        arrivals.append(remote(tpay, tp_ref.at[p], (leaf, p ^ k)))
        arrivals.append(remote(tc_ref, tcg_ref.at[p], (leaf, p ^ k)))
    for k in range(1, LEAFS):
        arrivals.append(remote(sc_ref, scg_ref.at[leaf], (leaf ^ k, p)))
    local(tpay, tp_ref.at[p])
    local(tc_ref, tcg_ref.at[p])
    local(sc_ref, scg_ref.at[leaf])


    @pl.loop(0, LEAVES)
    def _(m):
        lanes = pl.ds(pl.multiple_of(m * LEAF, LEAF), LEAF)
        prepare(m + 1, vec_ref[:, lanes], pts_ref[:, lanes])

    near_span(2, 6)
    step_c(-1)
    near_span(6, 10)
    step_c(1)
    near_span(10, 12)
    step_c(2)
    upper_levels(tops)
    near_span(12, 16)
    sibling_fields()
    h0.wait_recv()
    h1.wait_recv()
    for side, slot, edge in ((0, 0, 0), (1, LEAVES + 1, 127)):
        vec = jnp.where(me == edge, 0.0, halo_dst[side, 0:VEC])
        prepare(slot, vec, halo_dst[side, VEC:VEC + 3])
    near(1)
    near(LEAVES)

    far = sf[UPPER - 1]
    for u in range(UPPER - 2, -1, -1):
        far = sf[u] + dot3(far, matrix(TREE[u] + own_node(u)), NN)
    far_ref[...] = far

    for c in arrivals:
        c.wait_recv()
    for c in last:
        c.wait_recv()
    for c in sends:
        c.wait_send()
    for c in locals_[7:]:
        c.wait()


def couple_kernel(
    g_hbm, tp_hbm, sc_hbm, tc_hbm, o_ref, g_ref, tp_ref, sc_ref, tc_ref, sem, ct, wt, ut, masks, sums, d_scr, k_scr, acc_a, acc_b, used,
):
    leaf = lax.axis_index("leaf")
    p = lax.axis_index("pts")
    lane = lax.broadcasted_iota(jnp.int32, (16, 128), 1)
    low = lax.broadcasted_iota(jnp.int32, (RANK, 128), 1) < RANK

    def rows_of(index, size):
        return pl.ds(pl.multiple_of(index * size, size), size)

    blocks = [pltpu.make_async_copy(g_hbm.at[s], g_ref.at[s], sem.at[s]) for s in range(LEAFS)]
    others = [
        pltpu.make_async_copy(a, b, sem.at[LEAFS + i])
        for i, (a, b) in enumerate(((tp_hbm, tp_ref), (sc_hbm, sc_ref), (tc_hbm, tc_ref)))
    ]
    for copy in blocks + others:
        copy.start()

    for q in range(4):
        masks[q] = (lane // VEC == q).astype(F32).astype(BF16)
    for q in range(2):
        masks[4 + q] = (lane // RANK == q).astype(F32).astype(BF16)
    r = lax.broadcasted_iota(jnp.int32, (512, 128), 0)
    c = lax.broadcasted_iota(jnp.int32, (512, 128), 1)
    sums[...] = jnp.logical_and(
        lax.rem(r, VEC) == lax.rem(c, VEC), r // 128 == c // VEC
    ).astype(F32).astype(BF16)

    def masked(x, m):
        return (x.reshape(-1, 16, 128) * masks[m][None]).reshape(x.shape)

    for copy in others:
        copy.wait()

    def fill(s, count):
        pltpu.make_async_copy(g_hbm.at[s], g_ref.at[s], sem.at[s]).wait()
        for d in range(PTS):
            for row in range(6):
                r = tc_ref[d, row, s * PTS + p]
                used[count] = sc_ref[s, row, leaf * PTS + d] + r
                count = count + (r < d * (NODES + 1) + NODES).astype(jnp.int32)
        for g in range(GROUPS):
            c = g_ref[s, g * RANK:(g + 1) * RANK, :]
            for j in range(2):
                h, l = split(pltpu.roll(c, RANK, 1) if j else c)
                rows = (s * GROUPS + g) * 2 + j
                ct[rows_of(rows, 2 * RANK), :] = jnp.concatenate([h, l], axis=0)
        for a in range(PAIRS):
            x = jnp.concatenate(
                [
                    g_ref[s, COEF_ROWS + c * PAIRS + a:COEF_ROWS + c * PAIRS + a + 1, :]
                    for c in range(3)
                ],
                axis=0,
            )
            w = forms(x)[1]
            for j in range(2):
                rows = (s * PAIRS + a) * 2 + j
                wt[rows_of(rows, DEPTH), :] = stack_w(
                    pltpu.roll(w, RANK, 1) if j else w
                ).astype(BF16)

        return count

    for i in range(BATCH):
        used[i] = NODES
    end = lax.fori_loop(0, LEAFS, fill, jnp.int32(BATCH))
    for i in range(2 * BATCH):
        used[end + i] = NODES
    k_scr[...] = jnp.zeros_like(k_scr)
    slot_a = lax.broadcasted_iota(jnp.int32, (RANK, 2 * DEPTH), 1) < DEPTH

    @pl.loop(0, PTS)
    def _(d):
        first = d * (NODES + 1)
        for a in range(PAIRS):
            t = stack_u(tp_ref[d, a * 8:(a + 1) * 8, :])
            rows = pl.ds(pl.multiple_of((first + 2 * a) * RANK, RANK), 2 * RANK)
            ut[rows, :] = jnp.concatenate([t, t], axis=0).T.astype(BF16)
        ut[rows_of(first + NODES, RANK), :] = jnp.zeros((RANK, 2 * DEPTH), BF16)
        rows = pl.ds(pl.multiple_of(first * RANK, RANK), (NODES + 1) * RANK)
        acc_a[rows, :] = jnp.zeros(((NODES + 1) * RANK, 128), F32)
        acc_b[rows, :] = jnp.zeros(((NODES + 1) * RANK, 128), F32)

    def step(g, carry):
        def entry(i):
            e = used[g * BATCH + i]
            return e >> 8, rows_of(e & 255, RANK)

        for t in range(LEAFS):
            na, ra = entry(BATCH + 2 * t)
            nb, rb = entry(BATCH + 2 * t + 1)
            u = jnp.where(slot_a, ut[ra, :], ut[rb, :])
            wa = masked(wt[rows_of(na, DEPTH), :], 4)
            wb = masked(wt[rows_of(nb ^ 1, DEPTH), :], 5)
            d_scr[t * RANK:(t + 1) * RANK] = dg(u, jnp.concatenate([wa, wb], axis=0), NN)
        for t in range(LEAFS):
            na, ra = entry(2 * t)
            nb, rb = entry(2 * t + 1)
            xa = masked(ct[rows_of(na >> 1, 2 * RANK), :], na & 1)
            xb = masked(ct[rows_of((nb >> 1) ^ 1, 2 * RANK), :], 2 + (nb & 1))
            high = jnp.concatenate([xa[:RANK], xb[:RANK]], axis=0)
            rest = jnp.concatenate([xa[RANK:], xb[RANK:]], axis=0)
            part = dg(
                k_scr[t * RANK:(t + 1) * RANK], jnp.concatenate([high, high, rest], axis=0), NN
            )
            acc_a[ra, :] += part
            acc_b[rb, :] += part
            h, l = split(matern(d_scr[t * RANK:(t + 1) * RANK]))
            k_scr[t * RANK:(t + 1) * RANK] = jnp.concatenate([h, l, h], axis=1)
        return carry

    lax.fori_loop(0, (end + BATCH - 1) // BATCH, step, 0)

    @pl.loop(0, PTS)
    def _(d):
        for g in range(GROUPS):
            parts = []
            for q in range(4):
                rows = rows_of(d * (NODES + 1) + 4 * g + q, RANK)
                parts.append(jnp.where(low, acc_a[rows, :], acc_b[rows, :]))
            h, l = split(jnp.concatenate(parts, axis=1))
            o_ref[d, g * RANK:(g + 1) * RANK, :] = dg(h, sums[...], NN) + dg(l, sums[...], NN)


def scatter_kernel(
    acc_hbm, far_hbm, lt_hbm, base_hbm, near_hbm, out_ref,
    acc_ref, far_ref, lt_ref, base_ref, near_ref, from_core, s1, s2, work, ssem, rsem, lsem,
):
    leaf = lax.axis_index("leaf")
    p = lax.axis_index("pts")
    x = p // 2
    core = lax.rem(p, 2)
    sister = (leaf, p ^ 1)

    own_blocks = {}
    steps = (2, 1, 3, 0)
    for st in steps:
        blk = lax.rem(x + st, 4) * 2 + core
        own_blocks[st] = pltpu.make_async_copy(acc_hbm.at[blk], acc_ref.at[st], lsem.at[st])
        own_blocks[st].start()
    others = [
        pltpu.make_async_copy(a, b, lsem.at[4 + i])
        for i, (a, b) in enumerate(
            ((far_hbm, far_ref), (lt_hbm, lt_ref), (base_hbm, base_ref), (near_hbm, near_ref))
        )
    ]
    for copy in others:
        copy.start()

    def dev(step):
        return (leaf, lax.rem(x + step + 4, 4) * 2 + core)

    barrier = pltpu.get_barrier_semaphore()
    for d in (sister, dev(1), dev(-1)):
        pl.semaphore_signal(barrier, inc=1, device_id=d, device_id_type=MESH)
    pl.semaphore_wait(barrier, 3)

    sends = []

    def remote(src, dst, device):
        i = len(sends)
        copy = pltpu.make_async_remote_copy(
            src_ref=src, dst_ref=dst, send_sem=ssem.at[i], recv_sem=rsem.at[i],
            device_id=device, device_id_type=MESH,
        )
        copy.start()
        sends.append(copy)
        return copy

    half = COEF_ROWS // 2
    first = {}
    for st in steps:
        xx = lax.rem(x + st, 4)
        first[st] = remote(acc_hbm.at[xx * 2 + 1 - core], from_core.at[st], sister)

    def summed(st):
        first[st].wait_recv()
        own_blocks[st].wait()
        return acc_ref[st] + from_core[st]

    work[0] = summed(2)
    a1 = remote(work.at[0, pl.ds(0, half)], s1.at[pl.ds(0, half)], dev(1))
    b1 = remote(work.at[0, pl.ds(half, half)], s1.at[pl.ds(half, half)], dev(-1))
    work[1] = summed(1)
    work[2] = summed(3)
    a1.wait_recv()
    work[1, 0:half] += s1[0:half]
    a2 = remote(work.at[1], s2.at[0], dev(1))
    b1.wait_recv()
    work[2, half:] += s1[half:]
    b2 = remote(work.at[2], s2.at[1], dev(-1))

    def down(node, n):
        return dot3(node, pair_matrix(lt_ref, n), NN)

    for copy in others:
        copy.wait()
    top = down(far_ref[...], 14)
    level2 = [down(top[:, :RANK], 12), down(top[:, RANK:], 13)]
    own = summed(0)
    a2.wait_recv()
    b2.wait_recv()
    work[3] = own + (s2[0] + s2[1])

    turned = [work[3, g * RANK:(g + 1) * RANK].T for g in range(GROUPS)]

    def coupling(a):
        t = turned[a // 2]
        r = (a % 2) * 2 * VEC
        return jnp.concatenate([t[r:r + VEC], t[r + VEC:r + 2 * VEC]], axis=1)

    pairs = [level2[i] + coupling(12 + i) for i in range(2)]
    pairs = [
        down(pairs[i // 2][:, (i % 2) * RANK:(i % 2 + 1) * RANK], 8 + i) + coupling(8 + i)
        for i in range(4)
    ]
    pairs = [
        down(pairs[i // 2][:, (i % 2) * RANK:(i % 2 + 1) * RANK], i) + coupling(i)
        for i in range(8)
    ]
    for m in range(LEAVES):
        c = pairs[m // 2][:, (m % 2) * RANK:(m % 2 + 1) * RANK]
        cols = slice(m * LEAF, (m + 1) * LEAF)
        out_ref[:, cols] = near_ref[:, cols] + dot3(c, base_ref[m], NN)
    for c in sends:
        c.wait_send()


def vmem():
    return pl.BlockSpec(memory_space=pltpu.VMEM)


def anywhere():
    return pl.BlockSpec(memory_space=pl.ANY)


def shape(*dims, dtype=F32):
    return jax.ShapeDtypeStruct(dims, dtype)


def on_device(
    vectors, points, leaf_bases, local_transfer, skel_points, up_transfer, up_points,
    source_ids, target_ids, live_counts,
):
    sources = jnp.swapaxes(source_ids[:, 0], 1, 2)
    targets = jnp.swapaxes(target_ids[:, 0], 1, 2)
    lt = local_transfer[0]
    up_rows = jnp.transpose(up_transfer, (1, 2, 0)).reshape(RANK * RANK, UPN)
    n_remote = 112

    gathered, near, far, tp, scg, tcg = pl.pallas_call(
        gather_kernel,
        out_shape=(
            shape(LEAFS, PAY_ROWS, 128), shape(VEC, LEAVES * LEAF), shape(VEC, RANK),
            shape(PTS, PAIRS * 8, 128), shape(LEAFS, 8, 128, dtype=jnp.int32),
            shape(PTS, 8, 128, dtype=jnp.int32),
        ),
        in_specs=[anywhere()] * 7 + [vmem()] * 3,
        out_specs=(vmem(),) * 6,
        scratch_shapes=[
            pltpu.VMEM((VEC, LEAVES * LEAF), F32),
            pltpu.VMEM((3, LEAVES * LEAF), F32),
            pltpu.VMEM((LEAVES, RANK, LEAF), F32),
            pltpu.VMEM((30, RANK, RANK), F32),
            pltpu.VMEM((3, PAIRS * 128), F32),
            pltpu.VMEM((3, UPN * RANK), F32),
            pltpu.VMEM((8, 128), jnp.int32),
            pltpu.VMEM((8, 128), jnp.int32),
            pltpu.VMEM((18 * LEAF, DEPTH), BF16),
            pltpu.VMEM((DEPTH, 18 * LEAF), BF16),
            pltpu.VMEM((2 * VEC, 18 * LEAF), BF16),
            pltpu.VMEM((2, VEC + 8, LEAF), F32),
            pltpu.VMEM((2, VEC + 8, LEAF), F32),
            pltpu.VMEM((PAY_ROWS, 128), F32),
            pltpu.VMEM((PAIRS * 8, 128), F32),
            pltpu.VMEM((RANK * RANK, UPN), F32),
            pltpu.VMEM((48 * RANK, RANK), F32),
            pltpu.VMEM((44, VEC, RANK), F32),
            pltpu.VMEM((UPPER, VEC, RANK), F32),
            pltpu.SemaphoreType.DMA((n_remote,)),
            pltpu.SemaphoreType.DMA((n_remote,)),
            pltpu.SemaphoreType.DMA((16,)),
        ],
        compiler_params=pltpu.CompilerParams(
            collective_id=0, has_side_effects=True, vmem_limit_bytes=63 << 20
        ),
    )(vectors, points, leaf_bases, lt, skel_points, up_rows, up_points, sources, targets, live_counts)

    partial = pl.pallas_call(
        couple_kernel,
        out_shape=shape(PTS, COEF_ROWS, 128),
        in_specs=[anywhere()] * 4,
        out_specs=vmem(),
        scratch_shapes=[
            pltpu.VMEM((LEAFS, PAY_ROWS, 128), F32),
            pltpu.VMEM((PTS, PAIRS * 8, 128), F32),
            pltpu.SMEM((LEAFS, 8, 128), jnp.int32),
            pltpu.SMEM((PTS, 8, 128), jnp.int32),
            pltpu.SemaphoreType.DMA((LEAFS + 3,)),
            pltpu.VMEM((LEAFS * GROUPS * 4 * RANK, 128), BF16),
            pltpu.VMEM((LEAFS * NODES * DEPTH, 128), BF16),
            pltpu.VMEM((PTS * (NODES + 1) * RANK, 2 * DEPTH), BF16),
            pltpu.VMEM((8, 16, 128), BF16),
            pltpu.VMEM((512, 128), BF16),
            pltpu.VMEM((LEAFS * RANK, 128), F32),
            pltpu.VMEM((LEAFS * RANK, 3 * 128), BF16),
            pltpu.VMEM((PTS * (NODES + 1) * RANK, 128), F32),
            pltpu.VMEM((PTS * (NODES + 1) * RANK, 128), F32),
            pltpu.SMEM((1024,), jnp.int32),
        ],
        compiler_params=pltpu.CompilerParams(vmem_limit_bytes=63 << 20),
    )(gathered, tp, scg, tcg)

    return pl.pallas_call(
        scatter_kernel,
        out_shape=shape(VEC, LEAVES * LEAF),
        in_specs=[anywhere()] * 5,
        out_specs=vmem(),
        scratch_shapes=[
            pltpu.VMEM((4, COEF_ROWS, 128), F32),
            pltpu.VMEM((VEC, RANK), F32),
            pltpu.VMEM((30, RANK, RANK), F32),
            pltpu.VMEM((LEAVES, RANK, LEAF), F32),
            pltpu.VMEM((VEC, LEAVES * LEAF), F32),
            pltpu.VMEM((4, COEF_ROWS, 128), F32),
            pltpu.VMEM((COEF_ROWS, 128), F32),
            pltpu.VMEM((2, COEF_ROWS, 128), F32),
            pltpu.VMEM((4, COEF_ROWS, 128), F32),
            pltpu.SemaphoreType.DMA((8,)),
            pltpu.SemaphoreType.DMA((8,)),
            pltpu.SemaphoreType.DMA((8,)),
        ],
        compiler_params=pltpu.CompilerParams(
            collective_id=1, has_side_effects=True, vmem_limit_bytes=63 << 20
        ),
    )(partial, far, lt, leaf_bases, near)


def solution(mesh):
    both = ("leaf", "pts")
    return jax.shard_map(
        on_device,
        mesh=mesh,
        in_specs=(
            P(None, both),
            P(None, both),
            P(both, None, None),
            P(both, None, None, None),
            P(None, both),
            P(),
            P(),
            P(None, both, None, None),
            P(None, both, None, None),
            P(None, both, None),
        ),
        out_specs=P(None, both),
        check_vma=False,
    )
```
